128 devices in a mesh: seq: 16 (over z, x), head: 8 (over y, core).
Axes of the slice: x: 4, y: 4, z: 4, core: 2. Of those that a mesh axis runs over, the one named last changes fastest.
Arguments:
- queries: float32 [16384, 4096], P('seq', 'head'), may hold values from -6 to 6
- keys: float32 [16384, 4096], P('seq', 'head'), may hold values from -6 to 6
- values: float32 [16384, 4096], P('seq', 'head'), may hold values from -6 to 6
- out_grad: float32 [16384, 4096], P('seq', 'head'), may hold values from -6 to 6
- inputs: float32 [16384, 4096], P('seq', 'head'), may hold values from -20 to 20
- row_state: float32 [8, 4096], P('head', 'seq'), may hold values from 0.2 to 5
- col_state: float32 [16, 4096], P('seq', 'head'), may hold values from 0.2 to 5
Outputs:
- query_grad: float32 [16384, 4096], P('seq', 'head')
- key_grad: float32 [16384, 4096], P('seq', 'head')
- update: float32 [4096, 4096], P('seq', 'head')
- row_next: float32 [8, 4096], P('head', 'seq')
- col_next: float32 [16, 4096], P('seq', 'head')
The draws below stay inside these ranges and needn't reach their ends.
All inputs are finite; a program needn't handle non-finite values.
Results may differ from the reference program's by a relative error of at most 0.0001.
Values sent between devices are 32-bit elements; how exact they have to be, the bound alone decides.
A program may use at most 128 MiB of HBM per device.

```python
import math
import jax
import jax.numpy as jnp
from jax import lax

HEADS = 32
HEAD_DIM = 128
D = 4096
TOKENS = 16384
OUT_BLK = 256
IN_BLK = 512
N_SEQ = 16
N_HEAD = 8


def draw_inputs(key, part):
    key_base, key_cols = jax.random.split(jax.random.fold_in(key, 17), 2)
    column_scale = 10.0 ** jax.random.uniform(key_cols, (1, D), jnp.float32, -0.5, 0.5)
    drawn = jax.random.normal(key_base, (TOKENS, D), jnp.float32) * column_scale
    return jnp.clip(drawn, -20.0, 20.0)


def steps_of(stream_key, extent, cuts, low, high):
    loudness, own = 1.0, jax.random.fold_in(stream_key, 6)
    for axis_at, shards_of in cuts:
        heights = jnp.exp(jax.random.uniform(jax.random.fold_in(own, axis_at), (shards_of,), jnp.float32, low / len(cuts), high / len(cuts)))
        loudness = loudness * jnp.repeat(heights, extent[axis_at] // shards_of).reshape([-1 if axis == axis_at else 1 for axis in range(len(extent))])
    return loudness


def gaussian(rng, dims, spread, reach, shards=(), held_as=jnp.bfloat16):
    values = spread * jax.random.normal(rng, dims, jnp.float32)
    if shards:
        values = values * steps_of(rng, dims, shards, -0.22, 0.18)
    return jnp.clip(values, -reach, reach).astype(held_as)


def setup_inputs(seed: int = 0) -> dict:
    streams_of = jax.random.split(jax.random.key(seed), 8)
    return {
        "queries": gaussian(streams_of[0], (TOKENS, D), 1.0, 6.0, ((0, 16), (1, 8)), jnp.float32),
        "keys": gaussian(streams_of[1], (TOKENS, D), 1.0, 6.0, ((0, 16), (1, 8)), jnp.float32),
        "values": gaussian(streams_of[2], (TOKENS, D), 1.0, 6.0, ((0, 16), (1, 8)), jnp.float32),
        "out_grad": gaussian(streams_of[3], (TOKENS, D), 1.0, 6.0, ((0, 16), (1, 8)), jnp.float32),
        "inputs": draw_inputs(jax.random.fold_in(streams_of[7], 71), 0),
        "row_state": jnp.clip(jnp.exp(math.log(5.0) - 3.218876 * jax.random.uniform(streams_of[5], (N_HEAD, D), jnp.float32) ** steps_of(streams_of[5], (N_HEAD, D), ((0, 8), (1, 16)), -0.2, 0.2)), 0.2, 5.0),
        "col_state": jnp.clip(jnp.exp(math.log(5.0) - 3.218876 * jax.random.uniform(streams_of[6], (N_SEQ, D), jnp.float32) ** steps_of(streams_of[6], (N_SEQ, D), ((0, 16), (1, 8)), -0.2, 0.2)), 0.2, 5.0),
    }


highest = lax.Precision.HIGHEST
moment_eps = 1e-06
decay_rate = 0.9

def causal_terms(left_rows, right_rows):
    blk_size = left_rows.shape[0]
    scores = jnp.einsum('thd,shd->hts', left_rows, right_rows, precision=highest)
    rows_idx = lax.broadcasted_iota(jnp.int32, (blk_size, blk_size), 0)
    cols_idx = lax.broadcasted_iota(jnp.int32, (blk_size, blk_size), 1)
    causal_mask = (cols_idx <= rows_idx).astype(jnp.float32)
    return scores * causal_mask[None]

def reference(queries, keys, values, out_grad, inputs, row_state, col_state):
    blk_size = min(512, TOKENS)
    num_blocks = TOKENS // blk_size
    attn_scale = 1.0 / jnp.sqrt(jnp.float32(HEAD_DIM * TOKENS))

    def split_blocks(array):
        return array.reshape(num_blocks, blk_size, HEADS, HEAD_DIM)
    query_blocks = split_blocks(queries)
    key_blocks = split_blocks(keys)
    value_blocks = split_blocks(values)
    grad_blocks = split_blocks(out_grad)

    def forward_step(state_sum, pieces):
        query_part, key_part, value_part, grad_part = pieces
        grad_value = causal_terms(grad_part, value_part)
        inner = jnp.einsum('hts,shd->thd', grad_value, key_part, precision=highest)
        carried = jnp.einsum('tha,hab->thb', grad_part, state_sum, precision=highest)
        new_state = state_sum + jnp.einsum('sha,shb->hab', value_part, key_part, precision=highest)
        return (new_state, attn_scale * (inner + carried))

    def reverse_step(state_sum, pieces):
        query_part, key_part, value_part, grad_part = pieces
        grad_value = causal_terms(grad_part, value_part)
        query_key = causal_terms(query_part, key_part)
        inner_key = jnp.einsum('hts,thd->shd', grad_value, query_part, precision=highest)
        inner_value = jnp.einsum('hts,thd->shd', query_key, grad_part, precision=highest)
        carried_key = jnp.einsum('shb,hab->sha', value_part, state_sum, precision=highest)
        carried_value = jnp.einsum('sha,hab->shb', key_part, state_sum, precision=highest)
        new_state = state_sum + jnp.einsum('tha,thb->hab', query_part, grad_part, precision=highest)
        return (new_state, (attn_scale * (inner_key + carried_key), attn_scale * (inner_value + carried_value)))
    zero_state = jnp.zeros((HEADS, HEAD_DIM, HEAD_DIM), jnp.float32)
    pieces = (query_blocks, key_blocks, value_blocks, grad_blocks)
    final_fwd, query_grad = lax.scan(forward_step, zero_state, pieces)
    final_rev, (key_grad, value_grad) = lax.scan(reverse_step, zero_state, pieces, reverse=True)
    query_grad = query_grad.reshape(TOKENS, D)
    key_grad = key_grad.reshape(TOKENS, D)
    value_grad = value_grad.reshape(TOKENS, D)
    weight_grad = jnp.dot(value_grad.T, inputs, precision=highest, preferred_element_type=jnp.float32)
    weight_grad = weight_grad / jnp.sqrt(jnp.float32(TOKENS))
    grad_tiles = weight_grad.reshape(N_SEQ, OUT_BLK, N_HEAD, IN_BLK)
    squares = grad_tiles * grad_tiles + moment_eps
    row_mean = jnp.transpose(lax.optimization_barrier(jnp.mean(squares, axis=3)), (2, 0, 1)).reshape(N_HEAD, D)
    col_mean = lax.optimization_barrier(jnp.mean(squares, axis=1)).reshape(N_SEQ, D)
    row_next = decay_rate * row_state + (1.0 - decay_rate) * row_mean
    col_next = decay_rate * col_state + (1.0 - decay_rate) * col_mean
    row_tiles = jnp.transpose(row_next.reshape(N_HEAD, N_SEQ, OUT_BLK), (1, 2, 0))
    row_average = lax.optimization_barrier(jnp.mean(row_tiles, axis=1, keepdims=True))
    col_tiles = col_next.reshape(N_SEQ, N_HEAD, IN_BLK)[:, None, :, :]
    second = row_tiles[:, :, :, None] * col_tiles / row_average[:, :, :, None]
    update = (grad_tiles / jnp.sqrt(second)).reshape(D, D)
    return (query_grad, key_grad, update, row_next, col_next)
```

```python
import functools

import jax
import jax.numpy as jnp
import numpy as np
from jax import lax
from jax.experimental import pallas as pl
from jax.experimental.pallas import tpu as pltpu
from jax.sharding import PartitionSpec as P

F32 = jnp.float32
BF16 = jnp.bfloat16
MESH = pl.DeviceIdType.MESH

HEAD_DIM = 128
TOK = 1024
HEADS = 4
CH = 256
NCH = TOK // CH
HALF = 256
MOMENT_EPS = 1e-06
DECAY = 0.9
ATTN_SCALE = float(np.float32(1.0) / np.sqrt(np.float32(128 * 16384)))

NN = (((1,), (0,)), ((), ()))
NT = (((1,), (1,)), ((), ()))

SLOT_DY = (3, 1, 2, 0)
JOBS = ((3, 0), (3, 1), (0, 0), (1, 1), (0, 1), (1, 0), (2, 0), (2, 1))


def dot(a, b, dims=NN):
    return lax.dot_general(a, b, dims, preferred_element_type=F32)


def split(a):
    hi = a.astype(BF16)
    lo = (a - hi.astype(F32)).astype(BF16)
    return hi, lo


def mm_nt(a, b):
    both = jnp.concatenate([a[0], a[1]], axis=1)
    twice = jnp.concatenate([b[0], b[0]], axis=1)
    return dot(both, twice, NT) + dot(a[0], b[1], NT)


def mm_nn(a, b):
    wide = jnp.concatenate([b[0], b[1]], axis=1)
    first = dot(a[0], wide)
    return first[:, :128] + first[:, 128:] + dot(a[1], b[0])


def mm_state(a, b):
    both = jnp.concatenate([a[0], a[1]], axis=1)
    wide = jnp.concatenate([b[0], b[1]], axis=1)
    out = dot(both, jnp.concatenate([wide, wide], axis=0))
    return out[:, :128] + out[:, 128:]


def mm3(a, b):
    return dot(a[0], b[0]) + dot(a[0], b[1]) + dot(a[1], b[0])


def kernel(
    q_hbm, k_hbm, v_hbm, g_hbm, x_hbm, rowst, colst,
    qg_hbm, kg_hbm, upd, rown, coln,
    io, qg, kg, vt, vthi, vtlo, xbuf, xhi, xlo,
    rev_c, fwd_c, tot, ex1, val, tz, ex2, enter, run,
    pbuf, rs1, rs2, rs3, rs4, wfin,
    ld_sem, xo_sem, xs_sem, xr_sem, es_sem, er_sem, vs_sem, vr_sem,
    rss_sem, rsr_sem, fs_sem, fr_sem, out_sem,
):
    sq = lax.axis_index("seq")
    hd = lax.axis_index("head")
    z, x = sq // 4, sq % 4
    y, c = hd // 2, hd % 2

    def at_x(d):
        return (z * 4 + (x + d) % 4, hd)

    def at_z(d):
        return (((z + d) % 4) * 4 + x, hd)

    def at_y(d):
        return (sq, ((y + d) % 4) * 2 + c)

    sibling = (sq, y * 2 + 1 - c)

    def remote(src, dst, send, recv, dev):
        return pltpu.make_async_remote_copy(
            src_ref=src, dst_ref=dst, send_sem=send, recv_sem=recv, device_id=dev, device_id_type=MESH
        )

    def load(n, h):
        src = (q_hbm, k_hbm, v_hbm, g_hbm)[n]
        return pltpu.make_async_copy(
            src.at[:, pl.ds(h * 128, 128)], io.at[n, h], ld_sem.at[n, h]
        )

    for n in (3, 0, 2, 1):
        for h in range(HEADS):
            load(n, h).start()

    barrier = pltpu.get_barrier_semaphore()

    def greet(dev):
        pl.semaphore_signal(barrier, inc=1, device_id=dev, device_id_type=MESH)

    for dev in (at_y(1), at_y(3), sibling):
        greet(dev)
    for d in (1, 2, 3):
        greet(at_x(d))
        greet(at_z(d))
    for zs in range(4):

        @pl.when(jnp.logical_or(z != zs, z != y))
        def _(zs=zs):
            greet((zs * 4 + x, z * 2 + c))

    pl.semaphore_wait(barrier, 12 + (z != y).astype(jnp.int32))

    cols = (pl.ds(0, HALF), pl.ds(HALF, HALF))
    x_up = [
        remote(x_hbm.at[:, cols[i]], xbuf.at[0, :, cols[i]], xs_sem.at[0, i], xr_sem.at[0, i], at_y(1))
        for i in (0, 1)
    ]
    x_down = [
        remote(x_hbm.at[:, cols[i]], xbuf.at[1, :, cols[i]], xs_sem.at[1, i], xr_sem.at[1, i], at_y(3))
        for i in (0, 1)
    ]
    x_up[0].start()
    x_down[1].start()
    x_up[1].start()
    x_down[0].start()
    x_fwd_up = remote(
        xbuf.at[0, :, cols[0]], xbuf.at[2, :, cols[0]], xs_sem.at[2, 0], xr_sem.at[2, 0], at_y(1)
    )
    x_fwd_down = remote(
        xbuf.at[1, :, cols[1]], xbuf.at[2, :, cols[1]], xs_sem.at[2, 1], xr_sem.at[2, 1], at_y(3)
    )
    x_own = pltpu.make_async_copy(x_hbm, xbuf.at[3], xo_sem)
    x_own.start()

    def ex_a(st, d):
        dst = (x + d) % 4
        return remote(tot.at[st, dst], ex1.at[st, d - 1], es_sem.at[st, 0, d - 1], er_sem.at[st, 0, d - 1], at_x(d))

    def ex_b(st, d):
        return remote(tz.at[st], ex2.at[st, d - 1], es_sem.at[st, 1, d - 1], er_sem.at[st, 1, d - 1], at_z(d))

    def ex_c(st, d):
        return remote(val.at[st, d], enter.at[st, x], es_sem.at[st, 2, d - 1], er_sem.at[st, 2, d - 1], at_x(d))

    def counts(st, source, target):
        reached = source > target if st == 0 else source < target
        return reached.astype(F32)

    def send_a(st):
        for d in (1, 2, 3):
            ex_a(st, d).start()

    def send_b(st):
        for d in (1, 2, 3):
            ex_a(st, d).wait_recv()
        parts = [tot[st, x]] + [ex1[st, d - 1] for d in (1, 2, 3)]
        tz[st] = parts[0] + parts[1] + parts[2] + parts[3]
        for d in (1, 2, 3):
            ex_b(st, d).start()
        for e in range(4):
            target = (x + e) % 4
            terms = [counts(st, (x + 4 - d) % 4, target) * parts[d] for d in range(4)]
            val[st, e] = terms[0] + terms[1] + terms[2] + terms[3]

    def send_c(st):
        for d in (1, 2, 3):
            ex_b(st, d).wait_recv()
        base = sum(counts(st, (z + 4 - d) % 4, z) * ex2[st, d - 1] for d in (1, 2, 3))
        for e in (1, 2, 3):
            val[st, e] = val[st, e] + base
            ex_c(st, e).start()
        enter[st, x] = val[st, 0] + base

    def recv_c(st):
        for d in (1, 2, 3):
            remote(
                val.at[st, d], enter.at[st, (x + 4 - d) % 4],
                es_sem.at[st, 2, d - 1], er_sem.at[st, 2, d - 1], at_x(d),
            ).wait_recv()

    def rows(ch):
        return pl.ds(pl.multiple_of(ch * CH, CH), CH)

    def rev_states(h, carry):
        load(3, h).wait()
        load(0, h).wait()
        total = jnp.zeros((128, 128), F32)
        for ch in range(NCH):
            gt = split(io[3, h, ch * CH : (ch + 1) * CH].T)
            part = mm_nn(gt, split(io[0, h, ch * CH : (ch + 1) * CH]))
            rev_c[h, ch] = part
            total = total + part
        tot[0, h] = total
        return carry

    def fwd_states(h, carry):
        load(2, h).wait()
        load(1, h).wait()
        total = jnp.zeros((128, 128), F32)
        for ch in range(NCH):
            vtr = split(io[2, h, ch * CH : (ch + 1) * CH].T)
            part = mm_nn(vtr, split(io[1, h, ch * CH : (ch + 1) * CH]))
            fwd_c[h, ch] = part
            total = total + part
        tot[1, h] = total
        return carry

    lax.fori_loop(0, HEADS, rev_states, 0)
    send_a(0)
    lax.fori_loop(0, HEADS, fwd_states, 0)
    send_a(1)

    row_at = lax.broadcasted_iota(jnp.int32, (CH, CH), 0)
    col_at = lax.broadcasted_iota(jnp.int32, (CH, CH), 1)

    def intra(i, carry):
        h, ch = i // NCH, i % NCH
        for when, step in ((2, functools.partial(send_b, 0)), (4, functools.partial(send_b, 1)),
                           (6, functools.partial(send_c, 0)), (8, functools.partial(send_c, 1))):
            pl.when(i == when)(step)
        qf, kf, vf, gf = (io[n, h, rows(ch)] for n in range(4))
        q, k, v, g = split(qf), split(kf), split(vf), split(gf)
        causal = col_at <= row_at
        gv = split(jnp.where(causal, mm_nt(g, v), 0.0))
        qg[h, rows(ch)] = mm_nn(gv, k)
        vg = split(jnp.where(row_at <= col_at, mm_nt(v, g), 0.0))
        kg[h, rows(ch)] = mm_nn(vg, q)
        qk = split(jnp.where(causal, mm_nt(q, k), 0.0))
        vt[c * HEADS + h, :, rows(ch)] = mm3(split(gf.T), qk)
        return carry

    lax.fori_loop(0, HEADS * NCH, intra, 0)

    recv_c(0)

    def vt_copy(h):
        at = c * HEADS + h
        return remote(vt.at[at], vt.at[at], vs_sem.at[h], vr_sem.at[h], sibling)

    def finish_values(h, carry):
        suffix = enter[0, h]
        at = c * HEADS + h
        for ch in reversed(range(NCH)):
            span = pl.ds(ch * CH, CH)
            more = mm_nt(split(suffix), split(io[1, h, span]))
            done = ATTN_SCALE * (vt[at, :, span] + more)
            vt[at, :, span] = done
            hi, lo = split(done)
            vthi[at, :, span] = hi
            vtlo[at, :, span] = lo
            suffix = suffix + rev_c[h, ch]
        vt_copy(h).start()
        return carry

    lax.fori_loop(0, HEADS, finish_values, 0)
    recv_c(1)

    def out_copy(n, h):
        dst = (qg_hbm, kg_hbm)[n]
        return pltpu.make_async_copy((qg, kg)[n].at[h], dst.at[:, pl.ds(h * 128, 128)], out_sem.at[n, h])

    def finish_keys(h):
        suffix = enter[0, h]
        for ch in reversed(range(NCH)):
            span = pl.ds(ch * CH, CH)
            kg[h, span] = ATTN_SCALE * (kg[h, span] + mm_state(split(io[2, h, span]), split(suffix)))
            suffix = suffix + rev_c[h, ch]

    def finish_queries(h):
        prefix = enter[1, h]
        for ch in range(NCH):
            span = pl.ds(ch * CH, CH)
            qg[h, span] = ATTN_SCALE * (qg[h, span] + mm_state(split(io[3, h, span]), split(prefix)))
            prefix = prefix + fwd_c[h, ch]

    def finish_rest(h, carry):
        finish_keys(h)
        finish_queries(h)
        return carry

    lax.fori_loop(0, HEADS, finish_rest, 0)
    for n in (0, 1):
        for h in range(HEADS):
            out_copy(n, h).start()

    def take_values(h, carry):
        at = (1 - c) * HEADS + h
        remote(vt.at[at], vt.at[at], vs_sem.at[h], vr_sem.at[h], sibling).wait_recv()
        hi, lo = split(vt[at])
        vthi[at] = hi
        vtlo[at] = lo
        return carry

    lax.fori_loop(0, HEADS, take_values, 0)

    def product(j):
        slot, half = JOBS[j]

        def cut(t, carry):
            hi, lo = split(xbuf[slot, rows(t), cols[half]])
            xhi[rows(t)] = hi
            xlo[rows(t)] = lo
            return carry

        lax.fori_loop(0, TOK // CH, cut, 0)

        def block(a, carry):
            left = (vthi[pl.ds(2 * a, 2)].reshape(256, TOK), vtlo[pl.ds(2 * a, 2)].reshape(256, TOK))
            out = mm3(left, (xhi[...], xlo[...])).reshape(4, 64, HALF)
            if half == 0:
                pbuf[j, a] = out
            else:
                for r in range(4):
                    pbuf[j, r, a] = out[r]
            return carry

        lax.fori_loop(0, 4, block, 0)

    first = ((x, at_x), (z, at_z))
    second = ((z, at_z), (x, at_x))

    def rs(j, n, src, dst, dev):
        return remote(src, dst, rss_sem.at[j, n], rsr_sem.at[j, n], dev)

    def ring1(j):
        m, at = first[JOBS[j][1]]
        far = (m + 2) % 4
        return (
            rs(j, 0, pbuf.at[j, far, 0:2], rs1.at[j, 0], at(1)),
            rs(j, 1, pbuf.at[j, far, 2:4], rs1.at[j, 1], at(3)),
        )

    def ring2(j):
        m, at = first[JOBS[j][1]]
        return (
            rs(j, 2, pbuf.at[j, (m + 1) % 4], rs2.at[j, 0], at(1)),
            rs(j, 3, pbuf.at[j, (m + 3) % 4], rs2.at[j, 1], at(3)),
        )

    def ring3(j):
        m, _ = first[JOBS[j][1]]
        n, at = second[JOBS[j][1]]
        far = (n + 2) % 4
        return (
            rs(j, 4, pbuf.at[j, m, far, 0:32], rs3.at[j, 0], at(1)),
            rs(j, 5, pbuf.at[j, m, far, 32:64], rs3.at[j, 1], at(3)),
        )

    def ring4(j):
        m, _ = first[JOBS[j][1]]
        n, at = second[JOBS[j][1]]
        return (
            rs(j, 6, pbuf.at[j, m, (n + 1) % 4], rs4.at[j, 0], at(1)),
            rs(j, 7, pbuf.at[j, m, (n + 3) % 4], rs4.at[j, 1], at(3)),
        )

    def final(j):
        slot, half = JOBS[j]
        m, _ = first[half]
        n, _ = second[half]
        target = (y + SLOT_DY[slot]) % 4
        return remote(
            pbuf.at[j, m, n], wfin.at[z, :, cols[half]], fs_sem.at[j], fr_sem.at[z, half],
            (y * 4 + x, target * 2 + c),
        )

    def stage1(j):
        for copy in ring1(j):
            copy.start()

    def stage2(j):
        m, _ = first[JOBS[j][1]]
        got, send = ring1(j), ring2(j)
        got[0].wait_recv()
        up = (m + 1) % 4
        pbuf[j, up, 0:2] = pbuf[j, up, 0:2] + rs1[j, 0]
        send[0].start()
        got[1].wait_recv()
        down = (m + 3) % 4
        pbuf[j, down, 2:4] = pbuf[j, down, 2:4] + rs1[j, 1]
        send[1].start()

    def stage3(j):
        m, _ = first[JOBS[j][1]]
        for copy in ring2(j):
            copy.wait_recv()
        pbuf[j, m] = pbuf[j, m] + (rs2[j, 0] + rs2[j, 1])
        for copy in ring3(j):
            copy.start()

    def stage4(j):
        m, _ = first[JOBS[j][1]]
        n, _ = second[JOBS[j][1]]
        got, send = ring3(j), ring4(j)
        got[0].wait_recv()
        up = (n + 1) % 4
        pbuf[j, m, up, 0:32] = pbuf[j, m, up, 0:32] + rs3[j, 0]
        send[0].start()
        got[1].wait_recv()
        down = (n + 3) % 4
        pbuf[j, m, down, 32:64] = pbuf[j, m, down, 32:64] + rs3[j, 1]
        send[1].start()

    def stage5(j):
        slot, half = JOBS[j]
        m, _ = first[half]
        n, _ = second[half]
        for copy in ring4(j):
            copy.wait_recv()
        pbuf[j, m, n] = pbuf[j, m, n] + (rs4[j, 0] + rs4[j, 1])
        if slot == 3:

            @pl.when(z != y)
            def _():
                final(j).start()

            @pl.when(z == y)
            def _():
                wfin[z, :, cols[half]] = pbuf[j, m, n]
        else:
            final(j).start()

    stages = (stage1, stage2, stage3, stage4, stage5)

    def arrive(j):
        slot, half = JOBS[j]
        if slot == 3:
            if half == 0:
                x_own.wait()
        elif slot == 0:
            x_up[half].wait_recv()
            if half == 0:
                x_fwd_up.start()
        elif slot == 1:
            x_down[half].wait_recv()
            if half == 1:
                x_fwd_down.start()
        else:
            (x_fwd_up, x_fwd_down)[half].wait_recv()

    def advance(jobs, extra):
        pending = []
        for step in range(len(jobs) + extra):
            if step < len(jobs):
                arrive(jobs[step])
                product(jobs[step])
                pending.append([jobs[step], 0])
            for item in reversed(pending):
                if item[1] < len(stages):
                    stages[item[1]](item[0])
                    item[1] += 1

    advance((0, 1, 2, 3, 4, 5), 4)
    advance((6, 7), 4)

    for half in (0, 1):
        for zs in range(4):

            @pl.when(jnp.logical_or(z != zs, z != y))
            def _(half=half, zs=zs):
                remote(
                    pbuf.at[0, 0, 0], wfin.at[zs, :, cols[half]], fs_sem.at[0], fr_sem.at[zs, half], sibling
                ).wait_recv()

    w = wfin[...].reshape(256, 512) / jnp.sqrt(F32(16384.0))
    squares = w * w + MOMENT_EPS
    row_mean = jnp.broadcast_to(jnp.mean(squares, axis=1, keepdims=True), (256, 128))
    col_mean = jnp.mean(squares, axis=0, keepdims=True)
    row_old = jnp.broadcast_to(rowst[...], (128, 256)).T
    row_new = DECAY * row_old + (1.0 - DECAY) * row_mean
    col_new = DECAY * colst[...] + (1.0 - DECAY) * col_mean
    rown[...] = row_new.T[0:1]
    coln[...] = col_new
    row_one = row_new[:, 0:1]
    average = jnp.mean(row_one, axis=0, keepdims=True)
    upd[...] = w * lax.rsqrt(row_one * col_new / average)

    for n in (0, 1):
        for h in range(HEADS):
            out_copy(n, h).wait()
    for st in (0, 1):
        for d in (1, 2, 3):
            ex_a(st, d).wait_send()
            ex_b(st, d).wait_send()
            ex_c(st, d).wait_send()
    for h in range(HEADS):
        vt_copy(h).wait_send()
    for copy in (*x_up, *x_down, x_fwd_up, x_fwd_down):
        copy.wait_send()
    for j in range(len(JOBS)):
        for ring in (ring1, ring2, ring3, ring4):
            for copy in ring(j):
                copy.wait_send()
        if JOBS[j][0] == 3:

            @pl.when(z != y)
            def _(j=j):
                final(j).wait_send()
        else:
            final(j).wait_send()


def shards(queries, keys, values, out_grad, inputs, row_state, col_state):
    hbm = pl.BlockSpec(memory_space=pl.ANY)
    vmem = pl.BlockSpec(memory_space=pltpu.VMEM)
    jobs = len(JOBS)
    dma = pltpu.SemaphoreType.DMA
    scratch = [
        pltpu.VMEM((4, HEADS, TOK, 128), F32),
        pltpu.VMEM((HEADS, TOK, 128), F32),
        pltpu.VMEM((HEADS, TOK, 128), F32),
        pltpu.VMEM((2 * HEADS, 128, TOK), F32),
        pltpu.VMEM((2 * HEADS, 128, TOK), BF16),
        pltpu.VMEM((2 * HEADS, 128, TOK), BF16),
        pltpu.VMEM((4, TOK, 512), F32),
        pltpu.VMEM((TOK, HALF), BF16),
        pltpu.VMEM((TOK, HALF), BF16),
        pltpu.VMEM((HEADS, NCH, 128, 128), F32),
        pltpu.VMEM((HEADS, NCH, 128, 128), F32),
        pltpu.VMEM((2, HEADS, 128, 128), F32),
        pltpu.VMEM((2, 3, 128, 128), F32),
        pltpu.VMEM((2, 4, 128, 128), F32),
        pltpu.VMEM((2, 128, 128), F32),
        pltpu.VMEM((2, 3, 128, 128), F32),
        pltpu.VMEM((2, HEADS, 128, 128), F32),
        pltpu.VMEM((8, 128), F32),
        pltpu.VMEM((jobs, 4, 4, 64, HALF), F32),
        pltpu.VMEM((jobs, 2, 2, 64, HALF), F32),
        pltpu.VMEM((jobs, 2, 4, 64, HALF), F32),
        pltpu.VMEM((jobs, 2, 32, HALF), F32),
        pltpu.VMEM((jobs, 2, 64, HALF), F32),
        pltpu.VMEM((4, 64, 512), F32),
        dma((4, HEADS)),
        dma,
        dma((3, 2)),
        dma((3, 2)),
        dma((2, 3, 3)),
        dma((2, 3, 3)),
        dma((HEADS,)),
        dma((HEADS,)),
        dma((jobs, 8)),
        dma((jobs, 8)),
        dma((jobs,)),
        dma((4, 2)),
        dma((2, HEADS)),
    ]
    return pl.pallas_call(
        kernel,
        out_shape=(
            jax.ShapeDtypeStruct((TOK, 512), F32),
            jax.ShapeDtypeStruct((TOK, 512), F32),
            jax.ShapeDtypeStruct((256, 512), F32),
            jax.ShapeDtypeStruct((1, 256), F32),
            jax.ShapeDtypeStruct((1, 512), F32),
        ),
        in_specs=[hbm] * 5 + [vmem] * 2,
        out_specs=(hbm, hbm, vmem, vmem, vmem),
        scratch_shapes=scratch,
        compiler_params=pltpu.CompilerParams(
            collective_id=0, has_side_effects=True, vmem_limit_bytes=60 * 1024 * 1024
        ),
        cost_estimate=pl.CostEstimate(flops=20_000_000_000, bytes_accessed=16_000_000, transcendentals=0),
    )(queries, keys, values, out_grad, inputs, row_state, col_state)


def solution(mesh):
    in_specs = (
        P("seq", "head"),
        P("seq", "head"),
        P("seq", "head"),
        P("seq", "head"),
        P("seq", "head"),
        P("head", "seq"),
        P("seq", "head"),
    )
    out_specs = (
        P("seq", "head"),
        P("seq", "head"),
        P("seq", "head"),
        P("head", "seq"),
        P("seq", "head"),
    )
    return jax.shard_map(shards, mesh=mesh, in_specs=in_specs, out_specs=out_specs, check_vma=False)
```

```python
import jax
import jax.numpy as jnp
import numpy as np
from jax import lax
from jax.experimental import pallas as pl
from jax.experimental.pallas import tpu as pltpu
from jax.sharding import PartitionSpec as P

F32 = jnp.float32
BF16 = jnp.bfloat16
MESH = pl.DeviceIdType.MESH

HEAD_DIM = 128
TOK = 1024
HEADS = 4
CH = 256
NCH = TOK // CH
PART = 128
MOMENT_EPS = 1e-06
DECAY = 0.9
ATTN_SCALE = float(np.float32(1.0) / np.sqrt(np.float32(128 * 16384)))

NN = (((1,), (0,)), ((), ()))
NT = (((1,), (1,)), ((), ()))

SLOT_DY = (3, 1, 2, 0)
STEPS = ((3, 0), (3, 1), (0, 0), (1, 0), (0, 1), (1, 1), (2, 0), (2, 1))
JOBS = 2 * len(STEPS)


def dot(a, b, dims=NN):
    return lax.dot_general(a, b, dims, preferred_element_type=F32)


def split(a):
    hi = a.astype(BF16)
    lo = (a - hi.astype(F32)).astype(BF16)
    return hi, lo


def mm_nt(a, b):
    both = jnp.concatenate([a[0], a[1]], axis=1)
    twice = jnp.concatenate([b[0], b[0]], axis=1)
    return dot(both, twice, NT) + dot(a[0], b[1], NT)


def mm_nn(a, b):
    wide = jnp.concatenate([b[0], b[1]], axis=1)
    first = dot(a[0], wide)
    return first[:, :128] + first[:, 128:] + dot(a[1], b[0])


def mm_state(a, b):
    both = jnp.concatenate([a[0], a[1]], axis=1)
    wide = jnp.concatenate([b[0], b[1]], axis=1)
    out = dot(both, jnp.concatenate([wide, wide], axis=0))
    return out[:, :128] + out[:, 128:]


def mm3(a, b):
    return dot(a[0], b[0]) + dot(a[0], b[1]) + dot(a[1], b[0])


def kernel(
    q_hbm, k_hbm, v_hbm, g_hbm, x_hbm,
    qg_hbm, kg_hbm, w_out,
    io, qg, kg, vt, vthi, vtlo, xbuf, xhi, xlo,
    rev_c, fwd_c, tot, ex1, val, tz, ex2, enter,
    pbuf, rs1, rs2, rs3, wfin,
    ld_sem, xo_sem, xs_sem, xr_sem, xf_sem, xg_sem, es_sem, er_sem, vs_sem, vr_sem,
    rss_sem, rsr_sem, fs_sem, fr_sem, out_sem,
):
    sq = lax.axis_index("seq")
    hd = lax.axis_index("head")
    z, x = sq // 4, sq % 4
    y, c = hd // 2, hd % 2

    def at_x(d):
        return (z * 4 + (x + d) % 4, hd)

    def at_z(d):
        return (((z + d) % 4) * 4 + x, hd)

    def at_y(d):
        return (sq, ((y + d) % 4) * 2 + c)

    sibling = (sq, y * 2 + 1 - c)

    def remote(src, dst, send, recv, dev):
        return pltpu.make_async_remote_copy(
            src_ref=src, dst_ref=dst, send_sem=send, recv_sem=recv, device_id=dev, device_id_type=MESH
        )

    def load(n, h):
        src = (q_hbm, k_hbm, v_hbm, g_hbm)[n]
        return pltpu.make_async_copy(
            src.at[:, pl.ds(h * 128, 128)], io.at[n, h], ld_sem.at[n, h]
        )

    barrier = pltpu.get_barrier_semaphore()

    def greet(dev):
        pl.semaphore_signal(barrier, inc=1, device_id=dev, device_id_type=MESH)

    for dev in (at_y(1), at_y(3), sibling):
        greet(dev)
    for d in (1, 2, 3):
        greet(at_x(d))
        greet(at_z(d))
    for zs in range(4):

        @pl.when(jnp.logical_or(z != zs, z != y))
        def _(zs=zs):
            greet((zs * 4 + x, z * 2 + c))

    for n in (3, 0, 2, 1):
        for h in range(HEADS):
            load(n, h).start()

    pl.semaphore_wait(barrier, 12 + (z != y).astype(jnp.int32))

    def cols(half, part):
        return pl.ds(half * 256 + part * PART, PART)

    def x_direct(up, half, part):
        at = cols(half, part)
        slot = 0 if up else 1
        return remote(
            x_hbm.at[:, at], xbuf.at[slot, :, at], xs_sem.at[slot, half, part], xr_sem.at[slot, half, part],
            at_y(1 if up else 3),
        )

    def x_forward(half, part, tok):
        at = cols(half, part)
        span = pl.ds(tok * (TOK // 2), TOK // 2)
        sem = 2 * tok + part
        return remote(
            xbuf.at[half, span, at], xbuf.at[2, span, at], xf_sem.at[half, sem], xg_sem.at[half, sem],
            at_y(1 if half == 0 else 3),
        )

    def forward(part):
        x_direct(True, 0, part).wait_recv()
        x_direct(False, 1, part).wait_recv()
        for tok in (0, 1):
            x_forward(0, part, tok).start()
            x_forward(1, part, tok).start()

    for part in (0, 1):
        x_direct(True, 0, part).start()
        x_direct(False, 1, part).start()
        x_direct(True, 1, part).start()
        x_direct(False, 0, part).start()
    x_own = pltpu.make_async_copy(x_hbm, xbuf.at[3], xo_sem)
    x_own.start()

    def ex_a(st, d):
        dst = (x + d) % 4
        return remote(tot.at[st, dst], ex1.at[st, d - 1], es_sem.at[st, 0, d - 1], er_sem.at[st, 0, d - 1], at_x(d))

    def ex_b(st, d):
        return remote(tz.at[st], ex2.at[st, d - 1], es_sem.at[st, 1, d - 1], er_sem.at[st, 1, d - 1], at_z(d))

    def ex_c(st, d):
        return remote(val.at[st, d], enter.at[st, x], es_sem.at[st, 2, d - 1], er_sem.at[st, 2, d - 1], at_x(d))

    def counts(st, source, target):
        reached = source > target if st == 0 else source < target
        return reached.astype(F32)

    def send_a(st):
        for d in (1, 2, 3):
            ex_a(st, d).start()

    def send_b(st):
        for d in (1, 2, 3):
            ex_a(st, d).wait_recv()
        parts = [tot[st, x]] + [ex1[st, d - 1] for d in (1, 2, 3)]
        tz[st] = parts[0] + parts[1] + parts[2] + parts[3]
        for d in (1, 2, 3):
            ex_b(st, d).start()
        for e in range(4):
            target = (x + e) % 4
            terms = [counts(st, (x + 4 - d) % 4, target) * parts[d] for d in range(4)]
            val[st, e] = terms[0] + terms[1] + terms[2] + terms[3]

    def send_c(st):
        for d in (1, 2, 3):
            ex_b(st, d).wait_recv()
        base = sum(counts(st, (z + 4 - d) % 4, z) * ex2[st, d - 1] for d in (1, 2, 3))
        for e in (1, 2, 3):
            val[st, e] = val[st, e] + base
            ex_c(st, e).start()
        enter[st, x] = val[st, 0] + base

    def recv_c(st):
        for d in (1, 2, 3):
            remote(
                val.at[st, d], enter.at[st, (x + 4 - d) % 4],
                es_sem.at[st, 2, d - 1], er_sem.at[st, 2, d - 1], at_x(d),
            ).wait_recv()

    def rows(ch):
        return pl.ds(pl.multiple_of(ch * CH, CH), CH)

    def rev_states(h, carry):
        load(3, h).wait()
        load(0, h).wait()
        total = jnp.zeros((128, 128), F32)
        for ch in range(NCH):
            gt = split(io[3, h, ch * CH : (ch + 1) * CH].T)
            part = mm_nn(gt, split(io[0, h, ch * CH : (ch + 1) * CH]))
            rev_c[h, ch] = part
            total = total + part
        tot[0, h] = total
        return carry

    def fwd_states(h, carry):
        load(2, h).wait()
        load(1, h).wait()
        total = jnp.zeros((128, 128), F32)
        for ch in range(NCH):
            vtr = split(io[2, h, ch * CH : (ch + 1) * CH].T)
            part = mm_nn(vtr, split(io[1, h, ch * CH : (ch + 1) * CH]))
            fwd_c[h, ch] = part
            total = total + part
        tot[1, h] = total
        return carry

    row_at = lax.broadcasted_iota(jnp.int32, (CH, CH), 0)
    col_at = lax.broadcasted_iota(jnp.int32, (CH, CH), 1)

    causal = col_at <= row_at

    def value_part(i, carry):
        h, ch = i // NCH, i % NCH
        qk = mm_nt(split(io[0, h, rows(ch)]), split(io[1, h, rows(ch)]))
        vt[c * HEADS + h, :, rows(ch)] = mm3(split(io[3, h, rows(ch)].T), split(jnp.where(causal, qk, 0.0)))
        return carry

    def other_part(i, carry):
        h, ch = i // NCH, i % NCH
        q, k, v, g = (split(io[n, h, rows(ch)]) for n in range(4))
        gv = split(jnp.where(causal, mm_nt(g, v), 0.0))
        qg[h, rows(ch)] = mm_nn(gv, k)
        vg = split(jnp.where(row_at <= col_at, mm_nt(v, g), 0.0))
        kg[h, rows(ch)] = mm_nn(vg, q)
        return carry

    def other_parts(low, high):
        lax.fori_loop(low * NCH, high * NCH, other_part, 0)

    def vt_copy(h):
        at = c * HEADS + h
        return remote(vt.at[at], vt.at[at], vs_sem.at[h], vr_sem.at[h], sibling)

    def finish_values(h, carry):
        suffix = enter[0, h]
        at = c * HEADS + h
        for ch in reversed(range(NCH)):
            span = pl.ds(ch * CH, CH)
            more = mm_nt(split(suffix), split(io[1, h, span]))
            done = ATTN_SCALE * (vt[at, :, span] + more)
            vt[at, :, span] = done
            hi, lo = split(done)
            vthi[at, :, span] = hi
            vtlo[at, :, span] = lo
            suffix = suffix + rev_c[h, ch]
        vt_copy(h).start()
        return carry


    def out_copy(n, h):
        dst = (qg_hbm, kg_hbm)[n]
        return pltpu.make_async_copy((qg, kg)[n].at[h], dst.at[:, pl.ds(h * 128, 128)], out_sem.at[n, h])

    def finish_keys(h):
        suffix = enter[0, h]
        for ch in reversed(range(NCH)):
            span = pl.ds(ch * CH, CH)
            kg[h, span] = ATTN_SCALE * (kg[h, span] + mm_state(split(io[2, h, span]), split(suffix)))
            suffix = suffix + rev_c[h, ch]

    def finish_queries(h):
        prefix = enter[1, h]
        for ch in range(NCH):
            span = pl.ds(ch * CH, CH)
            qg[h, span] = ATTN_SCALE * (qg[h, span] + mm_state(split(io[3, h, span]), split(prefix)))
            prefix = prefix + fwd_c[h, ch]

    def finish_rest(h, carry):
        finish_keys(h)
        finish_queries(h)
        out_copy(0, h).start()
        out_copy(1, h).start()
        return carry


    def take_values(h, carry):
        at = (1 - c) * HEADS + h
        remote(vt.at[at], vt.at[at], vs_sem.at[h], vr_sem.at[h], sibling).wait_recv()
        hi, lo = split(vt[at])
        vthi[at] = hi
        vtlo[at] = lo
        return carry


    def product(p, toks=(0, 1)):
        slot, part = STEPS[p]
        span = pl.ds(toks[0] * (TOK // 2), len(toks) * (TOK // 2))

        def cut(t, carry):
            both = [xbuf[slot, rows(t), cols(half, part)] for half in (0, 1)]
            hi, lo = split(jnp.concatenate(both, axis=1))
            xhi[rows(t)] = hi
            xlo[rows(t)] = lo
            return carry

        lax.fori_loop(2 * toks[0], 2 * toks[-1] + 2, cut, 0)

        def block(a, carry):
            left = tuple(part[pl.ds(4 * a, 4), :, span].reshape(512, -1) for part in (vthi, vtlo))
            out = mm3(left, (xhi[span], xlo[span]))
            for b in (0, 1):
                near = out[b * 256 : (b + 1) * 256, :PART].reshape(4, 64, PART)
                at = 2 * a + b
                if toks[0] == 0:
                    pbuf[2 * p, at] = near
                else:
                    pbuf[2 * p, at] = pbuf[2 * p, at] + near
                for r in range(4):
                    far = out[b * 256 + r * 64 : b * 256 + (r + 1) * 64, PART:]
                    if toks[0] == 0:
                        pbuf[2 * p + 1, r, at] = far
                    else:
                        pbuf[2 * p + 1, r, at] = pbuf[2 * p + 1, r, at] + far
            return carry

        lax.fori_loop(0, 2, block, 0)

    first = ((x, at_x), (z, at_z))
    second = ((z, at_z), (x, at_x))

    def rs(j, n, src, dst, dev):
        return remote(src, dst, rss_sem.at[j, n], rsr_sem.at[j, n], dev)

    def ring1(j):
        m, at = first[j % 2]
        far = (m + 2) % 4
        return (
            rs(j, 0, pbuf.at[j, far, 0:2], rs1.at[j, 0], at(1)),
            rs(j, 1, pbuf.at[j, far, 2:4], rs1.at[j, 1], at(3)),
        )

    def ring2(j):
        m, at = first[j % 2]
        return (
            rs(j, 2, pbuf.at[j, (m + 1) % 4], rs2.at[j, 0], at(1)),
            rs(j, 3, pbuf.at[j, (m + 3) % 4], rs2.at[j, 1], at(3)),
        )

    def spread(j):
        m, _ = first[j % 2]
        n, at = second[j % 2]
        return tuple(
            rs(j, 3 + d, pbuf.at[j, m, (n + d) % 4], rs3.at[j, d - 1], at(d)) for d in (1, 2, 3)
        )

    def final(j):
        slot, part = STEPS[j // 2]
        half = j % 2
        m, _ = first[half]
        n, _ = second[half]
        target = (y + SLOT_DY[slot]) % 4
        return remote(
            pbuf.at[j, m, n], wfin.at[z, :, cols(half, part)], fs_sem.at[j], fr_sem.at[z, half, part],
            (y * 4 + x, target * 2 + c),
        )

    def stage1(j):
        for copy in ring1(j):
            copy.start()

    def stage2(j):
        m, _ = first[j % 2]
        got, send = ring1(j), ring2(j)
        got[0].wait_recv()
        up = (m + 1) % 4
        pbuf[j, up, 0:2] = pbuf[j, up, 0:2] + rs1[j, 0]
        send[0].start()
        got[1].wait_recv()
        down = (m + 3) % 4
        pbuf[j, down, 2:4] = pbuf[j, down, 2:4] + rs1[j, 1]
        send[1].start()

    def stage3(j):
        m, _ = first[j % 2]
        for copy in ring2(j):
            copy.wait_recv()
        pbuf[j, m] = pbuf[j, m] + (rs2[j, 0] + rs2[j, 1])
        for copy in spread(j):
            copy.start()

    def stage4(j):
        slot, part = STEPS[j // 2]
        half = j % 2
        m, _ = first[half]
        n, _ = second[half]
        for copy in spread(j):
            copy.wait_recv()
        pbuf[j, m, n] = (pbuf[j, m, n] + rs3[j, 0]) + (rs3[j, 1] + rs3[j, 2])
        if slot == 3:

            @pl.when(z != y)
            def _():
                final(j).start()

            @pl.when(z == y)
            def _():
                wfin[z, :, cols(half, part)] = pbuf[j, m, n]
        else:
            final(j).start()

    stages = (stage1, stage2, stage3, stage4)

    def stage(k, p):
        for half in (0, 1):
            stages[k - 1](2 * p + half)

    def arrive(p, toks=(0, 1)):
        slot, part = STEPS[p]
        if slot == 3:
            if part == 0:
                x_own.wait()
        elif slot == 2:
            for tok in toks:
                for half in (0, 1):
                    x_forward(half, part, tok).wait_recv()
        else:
            x_direct(slot == 0, 1 - slot, part).wait_recv()

    lax.fori_loop(0, HEADS, rev_states, 0)
    send_a(0)
    lax.fori_loop(0, HEADS, fwd_states, 0)
    send_b(0)
    send_a(1)
    lax.fori_loop(0, HEADS * NCH, value_part, 0)
    send_c(0)
    send_b(1)
    other_parts(0, 2)
    recv_c(0)
    lax.fori_loop(0, HEADS, finish_values, 0)
    send_c(1)
    forward(0)
    lax.fori_loop(0, HEADS, take_values, 0)

    def step(p):
        arrive(p)
        product(p)
        stage(1, p)

    def finish(low, high):
        lax.fori_loop(low, high, finish_rest, 0)

    step(0)
    step(1)
    step(2)
    stage(2, 0)
    stage(2, 1)
    step(3)
    stage(3, 0)
    stage(2, 2)
    stage(3, 1)
    forward(1)
    other_parts(2, 3)
    stage(4, 0)
    stage(2, 3)
    stage(3, 2)
    other_parts(3, 4)
    stage(4, 1)
    stage(3, 3)
    step(4)
    stage(4, 2)
    step(5)
    stage(2, 4)
    stage(4, 3)
    recv_c(1)
    finish(0, 2)
    stage(2, 5)
    step(6)
    stage(3, 4)
    stage(3, 5)
    stage(2, 6)
    finish(2, 4)
    stage(4, 4)
    stage(4, 5)
    stage(3, 6)
    arrive(7, (0,))
    product(7, (0,))
    stage(4, 6)
    arrive(7, (1,))
    product(7, (1,))
    stage(1, 7)
    stage(2, 7)
    stage(3, 7)
    stage(4, 7)

    for part in range(4):
        for zs in range(4):

            @pl.when(jnp.logical_or(z != zs, z != y))
            def _(part=part, zs=zs):
                at = cols(part // 2, part % 2)
                sem = fr_sem.at[zs, part // 2, part % 2]
                remote(pbuf.at[0, 0, 0], wfin.at[zs, :, at], fs_sem.at[0], sem, sibling).wait_recv()

    w_out[...] = wfin[...].reshape(256, 512)

    for n in (0, 1):
        for h in range(HEADS):
            out_copy(n, h).wait()
    for st in (0, 1):
        for d in (1, 2, 3):
            ex_a(st, d).wait_send()
            ex_b(st, d).wait_send()
            ex_c(st, d).wait_send()
    for h in range(HEADS):
        vt_copy(h).wait_send()
    for half in (0, 1):
        for part in (0, 1):
            x_direct(True, half, part).wait_send()
            x_direct(False, half, part).wait_send()
            x_forward(half, part, 0).wait_send()
            x_forward(half, part, 1).wait_send()
    for j in range(JOBS):
        for ring in (ring1, ring2, spread):
            for copy in ring(j):
                copy.wait_send()
        if STEPS[j // 2][0] == 3:

            @pl.when(z != y)
            def _(j=j):
                final(j).wait_send()
        else:
            final(j).wait_send()


def last_kernel(qg_in, kg_in, w_in, rowst, colst, qg_out, kg_out, upd, rown, coln, stage, sem):
    pieces = [(n, i) for n in (0, 1) for i in range(4)]

    def load(n, i):
        return pltpu.make_async_copy((qg_in, kg_in)[n].at[pl.ds(i * 256, 256)], stage.at[n, i], sem.at[0, n, i])

    def store(n, i):
        return pltpu.make_async_copy(stage.at[n, i], (qg_out, kg_out)[n].at[pl.ds(i * 256, 256)], sem.at[1, n, i])

    for piece in pieces:
        load(*piece).start()
    for piece in pieces:
        load(*piece).wait()
        store(*piece).start()
    w = w_in[...] / jnp.sqrt(F32(16384.0))
    squares = w * w + MOMENT_EPS
    row_mean = jnp.broadcast_to(jnp.mean(squares, axis=1, keepdims=True), (256, 128))
    col_mean = jnp.mean(squares, axis=0, keepdims=True)
    row_old = jnp.broadcast_to(rowst[...], (128, 256)).T
    row_new = DECAY * row_old + (1.0 - DECAY) * row_mean
    col_new = DECAY * colst[...] + (1.0 - DECAY) * col_mean
    rown[...] = row_new.T[0:1]
    coln[...] = col_new
    row_one = row_new[:, 0:1]
    average = jnp.mean(row_one, axis=0, keepdims=True)
    upd[...] = w * lax.rsqrt(row_one * col_new / average)
    for piece in pieces:
        store(*piece).wait()


def shards(queries, keys, values, out_grad, inputs, row_state, col_state):
    hbm = pl.BlockSpec(memory_space=pl.ANY)
    vmem = pl.BlockSpec(memory_space=pltpu.VMEM)
    dma = pltpu.SemaphoreType.DMA
    scratch = [
        pltpu.VMEM((4, HEADS, TOK, 128), F32),
        pltpu.VMEM((HEADS, TOK, 128), F32),
        pltpu.VMEM((HEADS, TOK, 128), F32),
        pltpu.VMEM((2 * HEADS, 128, TOK), F32),
        pltpu.VMEM((2 * HEADS, 128, TOK), BF16),
        pltpu.VMEM((2 * HEADS, 128, TOK), BF16),
        pltpu.VMEM((4, TOK, 512), F32),
        pltpu.VMEM((TOK, 2 * PART), BF16),
        pltpu.VMEM((TOK, 2 * PART), BF16),
        pltpu.VMEM((HEADS, NCH, 128, 128), F32),
        pltpu.VMEM((HEADS, NCH, 128, 128), F32),
        pltpu.VMEM((2, HEADS, 128, 128), F32),
        pltpu.VMEM((2, 3, 128, 128), F32),
        pltpu.VMEM((2, 4, 128, 128), F32),
        pltpu.VMEM((2, 128, 128), F32),
        pltpu.VMEM((2, 3, 128, 128), F32),
        pltpu.VMEM((2, HEADS, 128, 128), F32),
        pltpu.VMEM((JOBS, 4, 4, 64, PART), F32),
        pltpu.VMEM((JOBS, 2, 2, 64, PART), F32),
        pltpu.VMEM((JOBS, 2, 4, 64, PART), F32),
        pltpu.VMEM((JOBS, 3, 64, PART), F32),
        pltpu.VMEM((4, 64, 512), F32),
        dma((4, HEADS)),
        dma,
        dma((2, 2, 2)),
        dma((2, 2, 2)),
        dma((2, 4)),
        dma((2, 4)),
        dma((2, 3, 3)),
        dma((2, 3, 3)),
        dma((HEADS,)),
        dma((HEADS,)),
        dma((JOBS, 7)),
        dma((JOBS, 7)),
        dma((JOBS,)),
        dma((4, 2, 2)),
        dma((2, HEADS)),
    ]
    tokens = jax.ShapeDtypeStruct((TOK, 512), F32)
    block = jax.ShapeDtypeStruct((256, 512), F32)
    query_grad, key_grad, weight_grad = pl.pallas_call(
        kernel,
        out_shape=(tokens, tokens, block),
        in_specs=[hbm] * 5,
        out_specs=(hbm, hbm, vmem),
        scratch_shapes=scratch,
        compiler_params=pltpu.CompilerParams(
            collective_id=0, has_side_effects=True, vmem_limit_bytes=60 * 1024 * 1024
        ),
        cost_estimate=pl.CostEstimate(flops=20_000_000_000, bytes_accessed=16_000_000, transcendentals=0),
    )(queries, keys, values, out_grad, inputs)
    return pl.pallas_call(
        last_kernel,
        out_shape=(
            tokens,
            tokens,
            block,
            jax.ShapeDtypeStruct((1, 256), F32),
            jax.ShapeDtypeStruct((1, 512), F32),
        ),
        in_specs=[hbm] * 2 + [vmem] * 3,
        out_specs=(hbm, hbm, vmem, vmem, vmem),
        scratch_shapes=[pltpu.VMEM((2, 4, 256, 512), F32), dma((2, 2, 4))],
        compiler_params=pltpu.CompilerParams(vmem_limit_bytes=60 * 1024 * 1024),
        cost_estimate=pl.CostEstimate(flops=2_000_000, bytes_accessed=10_000_000, transcendentals=131072),
    )(query_grad, key_grad, weight_grad, row_state, col_state)


def solution(mesh):
    in_specs = (
        P("seq", "head"),
        P("seq", "head"),
        P("seq", "head"),
        P("seq", "head"),
        P("seq", "head"),
        P("head", "seq"),
        P("seq", "head"),
    )
    out_specs = (
        P("seq", "head"),
        P("seq", "head"),
        P("seq", "head"),
        P("head", "seq"),
        P("seq", "head"),
    )
    return jax.shard_map(shards, mesh=mesh, in_specs=in_specs, out_specs=out_specs, check_vma=False)
```

```python
import jax
import jax.numpy as jnp
import numpy as np
from jax import lax
from jax.experimental import pallas as pl
from jax.experimental.pallas import tpu as pltpu
from jax.sharding import PartitionSpec as P

F32 = jnp.float32
BF16 = jnp.bfloat16
MESH = pl.DeviceIdType.MESH

HEAD_DIM = 128
TOK = 1024
HEADS = 4
CH = 256
NCH = TOK // CH
PART = 128
MOMENT_EPS = 1e-06
DECAY = 0.9
ATTN_SCALE = float(np.float32(1.0) / np.sqrt(np.float32(128 * 16384)))

NN = (((1,), (0,)), ((), ()))
NT = (((1,), (1,)), ((), ()))

SLOT_DY = (3, 1, 2, 0)
STEPS = ((3, 0), (3, 1), (0, 0), (1, 0), (0, 1), (1, 1), (2, 0), (2, 1))
JOBS = 2 * len(STEPS)
RINGED = 6


def dot(a, b, dims=NN):
    return lax.dot_general(a, b, dims, preferred_element_type=F32)


def split(a):
    hi = a.astype(BF16)
    lo = (a - hi.astype(F32)).astype(BF16)
    return hi, lo


def mm_nt(a, b):
    both = jnp.concatenate([a[0], a[1]], axis=1)
    twice = jnp.concatenate([b[0], b[0]], axis=1)
    return dot(both, twice, NT) + dot(a[0], b[1], NT)


def mm_nn(a, b):
    wide = jnp.concatenate([b[0], b[1]], axis=1)
    first = dot(a[0], wide)
    return first[:, :128] + first[:, 128:] + dot(a[1], b[0])


def mm_state(a, b):
    both = jnp.concatenate([a[0], a[1]], axis=1)
    wide = jnp.concatenate([b[0], b[1]], axis=1)
    out = dot(both, jnp.concatenate([wide, wide], axis=0))
    return out[:, :128] + out[:, 128:]


def mm3(a, b):
    return dot(a[0], b[0]) + dot(a[0], b[1]) + dot(a[1], b[0])


def kernel(
    q_hbm, k_hbm, v_hbm, g_hbm, x_hbm,
    qg_hbm, kg_hbm, w_out,
    io, qg, kg, vt, vtc, xbuf, xc,
    rev_c, fwd_c, tot, ex1, val, tz, ex2, enter,
    pbuf, rs1, rs2, rs3, rs4, wfin,
    ld_sem, xo_sem, xs_sem, xr_sem, xf_sem, xg_sem, es_sem, er_sem, vs_sem, vr_sem,
    rss_sem, rsr_sem, fs_sem, fr_sem, out_sem,
):
    sq = lax.axis_index("seq")
    hd = lax.axis_index("head")
    z, x = sq // 4, sq % 4
    y, c = hd // 2, hd % 2

    x_at = [x] + [(x + d) % 4 for d in (1, 2, 3)]
    z_at = [z] + [(z + d) % 4 for d in (1, 2, 3)]
    y_at = [y] + [(y + d) % 4 for d in (1, 2, 3)]
    x_ids = [z * 4 + x_at[d] for d in range(4)]
    z_ids = [z_at[d] * 4 + x for d in range(4)]
    y_ids = [y_at[d] * 2 + c for d in range(4)]
    last_seq = y * 4 + x

    def at_x(d):
        return (x_ids[d], hd)

    def at_z(d):
        return (z_ids[d], hd)

    def at_y(d):
        return (sq, y_ids[d])

    sibling = (sq, y * 2 + 1 - c)

    def remote(src, dst, send, recv, dev):
        return pltpu.make_async_remote_copy(
            src_ref=src, dst_ref=dst, send_sem=send, recv_sem=recv, device_id=dev, device_id_type=MESH
        )

    def load(n, h):
        src = (q_hbm, k_hbm, v_hbm, g_hbm)[n]
        return pltpu.make_async_copy(
            src.at[:, pl.ds(h * 128, 128)], io.at[n, h], ld_sem.at[n, h]
        )

    barrier = pltpu.get_barrier_semaphore()

    def greet(dev):
        pl.semaphore_signal(barrier, inc=1, device_id=dev, device_id_type=MESH)

    for dev in (at_y(1), at_y(3), sibling):
        greet(dev)
    for d in (1, 2, 3):
        greet(at_x(d))
        greet(at_z(d))
    for zs in range(4):

        @pl.when(jnp.logical_or(z != zs, z != y))
        def _(zs=zs):
            greet((zs * 4 + x, z * 2 + c))

    for n in (3, 0, 2, 1):
        for h in range(HEADS):
            load(n, h).start()

    pl.semaphore_wait(barrier, 12 + (z != y).astype(jnp.int32))

    def cols(half, part):
        return pl.ds(half * 256 + part * PART, PART)

    def x_direct(up, half, part):
        at = cols(half, part)
        slot = 0 if up else 1
        return remote(
            x_hbm.at[:, at], xbuf.at[slot, :, at], xs_sem.at[slot, half, part], xr_sem.at[slot, half, part],
            at_y(1 if up else 3),
        )

    def x_forward(half, part, tok):
        at = cols(half, part)
        span = pl.ds(tok * (TOK // 2), TOK // 2)
        sem = 2 * tok + part
        return remote(
            xbuf.at[half, span, at], xbuf.at[2, span, at], xf_sem.at[half, sem], xg_sem.at[half, sem],
            at_y(1 if half == 0 else 3),
        )

    def forward(part):
        x_direct(True, 0, part).wait_recv()
        x_direct(False, 1, part).wait_recv()
        for tok in (0, 1):
            x_forward(0, part, tok).start()
            x_forward(1, part, tok).start()

    for part in (0, 1):
        x_direct(True, 0, part).start()
        x_direct(False, 1, part).start()
        x_direct(True, 1, part).start()
        x_direct(False, 0, part).start()
    x_own = pltpu.make_async_copy(x_hbm, xbuf.at[3], xo_sem)
    x_own.start()

    def ex_a(st, d):
        dst = (x + d) % 4
        return remote(tot.at[st, dst], ex1.at[st, d - 1], es_sem.at[st, 0, d - 1], er_sem.at[st, 0, d - 1], at_x(d))

    def ex_b(st, d):
        return remote(tz.at[st], ex2.at[st, d - 1], es_sem.at[st, 1, d - 1], er_sem.at[st, 1, d - 1], at_z(d))

    def ex_c(st, d):
        return remote(val.at[st, d], enter.at[st, x], es_sem.at[st, 2, d - 1], er_sem.at[st, 2, d - 1], at_x(d))

    def counts(st, source, target):
        reached = source > target if st == 0 else source < target
        return reached.astype(F32)

    def send_a(st):
        for d in (1, 2, 3):
            ex_a(st, d).start()

    def send_b(st):
        for d in (1, 2, 3):
            ex_a(st, d).wait_recv()
        parts = [tot[st, x]] + [ex1[st, d - 1] for d in (1, 2, 3)]
        tz[st] = parts[0] + parts[1] + parts[2] + parts[3]
        for d in (1, 2, 3):
            ex_b(st, d).start()
        for e in range(4):
            target = (x + e) % 4
            terms = [counts(st, (x + 4 - d) % 4, target) * parts[d] for d in range(4)]
            val[st, e] = terms[0] + terms[1] + terms[2] + terms[3]

    def send_c(st):
        for d in (1, 2, 3):
            ex_b(st, d).wait_recv()
        base = sum(counts(st, (z + 4 - d) % 4, z) * ex2[st, d - 1] for d in (1, 2, 3))
        for e in (1, 2, 3):
            val[st, e] = val[st, e] + base
            ex_c(st, e).start()
        enter[st, x] = val[st, 0] + base

    def recv_c(st):
        for d in (1, 2, 3):
            remote(
                val.at[st, d], enter.at[st, (x + 4 - d) % 4],
                es_sem.at[st, 2, d - 1], er_sem.at[st, 2, d - 1], at_x(d),
            ).wait_recv()

    def rows(ch):
        return pl.ds(pl.multiple_of(ch * CH, CH), CH)

    def rev_states(h, carry):
        load(3, h).wait()
        load(0, h).wait()
        total = jnp.zeros((128, 128), F32)
        for ch in range(NCH):
            gt = split(io[3, h, ch * CH : (ch + 1) * CH].T)
            part = mm_nn(gt, split(io[0, h, ch * CH : (ch + 1) * CH]))
            rev_c[h, ch] = part
            total = total + part
        tot[0, h] = total
        return carry

    def fwd_states(h, carry):
        load(2, h).wait()
        load(1, h).wait()
        total = jnp.zeros((128, 128), F32)
        for ch in range(NCH):
            vtr = split(io[2, h, ch * CH : (ch + 1) * CH].T)
            part = mm_nn(vtr, split(io[1, h, ch * CH : (ch + 1) * CH]))
            fwd_c[h, ch] = part
            total = total + part
        tot[1, h] = total
        return carry

    row_at = lax.broadcasted_iota(jnp.int32, (CH, CH), 0)
    col_at = lax.broadcasted_iota(jnp.int32, (CH, CH), 1)

    causal = col_at <= row_at

    def value_part(i, carry):
        h, ch = i // NCH, i % NCH
        qk = mm_nt(split(io[0, h, rows(ch)]), split(io[1, h, rows(ch)]))
        vt[c * HEADS + h, :, rows(ch)] = mm3(split(io[3, h, rows(ch)].T), split(jnp.where(causal, qk, 0.0)))
        return carry

    def other_part(i, carry):
        h, ch = i // NCH, i % NCH
        q, k, v, g = (split(io[n, h, rows(ch)]) for n in range(4))
        gv = split(jnp.where(causal, mm_nt(g, v), 0.0))
        qg[h, rows(ch)] = mm_nn(gv, k)
        vg = split(jnp.where(row_at <= col_at, mm_nt(v, g), 0.0))
        kg[h, rows(ch)] = mm_nn(vg, q)
        return carry

    def other_parts(low, high):
        lax.fori_loop(low * NCH, high * NCH, other_part, 0)

    def vt_copy(h):
        at = c * HEADS + h
        return remote(vt.at[at], vt.at[at], vs_sem.at[h], vr_sem.at[h], sibling)

    def finish_values(h, carry):
        suffix = enter[0, h]
        at = c * HEADS + h
        for ch in reversed(range(NCH)):
            span = pl.ds(ch * CH, CH)
            more = mm_nt(split(suffix), split(io[1, h, span]))
            done = ATTN_SCALE * (vt[at, :, span] + more)
            vt[at, :, span] = done
            hi, lo = split(done)
            vtc[at, :, span] = hi
            vtc[at, :, pl.ds(TOK + ch * CH, CH)] = lo
            vtc[at, :, pl.ds(2 * TOK + ch * CH, CH)] = hi
            suffix = suffix + rev_c[h, ch]
        vt_copy(h).start()
        return carry


    def out_copy(n, h):
        dst = (qg_hbm, kg_hbm)[n]
        return pltpu.make_async_copy((qg, kg)[n].at[h], dst.at[:, pl.ds(h * 128, 128)], out_sem.at[n, h])

    def finish_keys(h):
        suffix = enter[0, h]
        for ch in reversed(range(NCH)):
            span = pl.ds(ch * CH, CH)
            kg[h, span] = ATTN_SCALE * (kg[h, span] + mm_state(split(io[2, h, span]), split(suffix)))
            suffix = suffix + rev_c[h, ch]

    def finish_queries(h):
        prefix = enter[1, h]
        for ch in range(NCH):
            span = pl.ds(ch * CH, CH)
            qg[h, span] = ATTN_SCALE * (qg[h, span] + mm_state(split(io[3, h, span]), split(prefix)))
            prefix = prefix + fwd_c[h, ch]

    def finish_rest(h, carry):
        finish_keys(h)
        finish_queries(h)
        out_copy(0, h).start()
        out_copy(1, h).start()
        return carry


    def take_values(h, carry):
        at = (1 - c) * HEADS + h
        remote(vt.at[at], vt.at[at], vs_sem.at[h], vr_sem.at[h], sibling).wait_recv()
        hi, lo = split(vt[at])
        vtc[at, :, 0:TOK] = hi
        vtc[at, :, TOK : 2 * TOK] = lo
        vtc[at, :, 2 * TOK : 3 * TOK] = hi
        return carry


    def product(p, toks=(0, 1)):
        slot, part = STEPS[p]

        def cut(t, carry):
            both = [xbuf[slot, rows(t), cols(half, part)] for half in (0, 1)]
            hi, lo = split(jnp.concatenate(both, axis=1))
            xc[rows(t)] = hi
            xc[rows(t + NCH)] = hi
            xc[rows(t + 2 * NCH)] = lo
            return carry

        lax.fori_loop(2 * toks[0], 2 * toks[-1] + 2, cut, 0)

        def block(a, carry):
            blocks = pl.ds(4 * a, 4)
            if len(toks) == 2:
                out = dot(vtc[blocks].reshape(512, 3 * TOK), xc[...])
            else:
                low = toks[0] * (TOK // 2)
                spans = [pl.ds(low + n * TOK, TOK // 2) for n in range(3)]
                out = sum(dot(vtc[blocks, :, span].reshape(512, TOK // 2), xc[span]) for span in spans)
            for b in (0, 1):
                near = out[b * 256 : (b + 1) * 256, :PART].reshape(4, 64, PART)
                at = 2 * a + b
                if toks[0] == 0:
                    pbuf[2 * p, at] = near
                else:
                    pbuf[2 * p, at] = pbuf[2 * p, at] + near
                for r in range(4):
                    far = out[b * 256 + r * 64 : b * 256 + (r + 1) * 64, PART:]
                    if toks[0] == 0:
                        pbuf[2 * p + 1, r, at] = far
                    else:
                        pbuf[2 * p + 1, r, at] = pbuf[2 * p + 1, r, at] + far
            return carry

        lax.fori_loop(0, 2, block, 0)

    first = ((x_at, at_x), (z_at, at_z))
    second = ((z_at, at_z), (x_at, at_x))

    def rs(j, n, src, dst, dev):
        return remote(src, dst, rss_sem.at[j, n], rsr_sem.at[j, n], dev)

    def ring1(j):
        m, at = first[j % 2]
        far = m[2]
        return (
            rs(j, 0, pbuf.at[j, far, 0:2], rs1.at[j, 0], at(1)),
            rs(j, 1, pbuf.at[j, far, 2:4], rs1.at[j, 1], at(3)),
        )

    def ring2(j):
        m, at = first[j % 2]
        return (
            rs(j, 2, pbuf.at[j, m[1]], rs2.at[j, 0], at(1)),
            rs(j, 3, pbuf.at[j, m[3]], rs2.at[j, 1], at(3)),
        )

    def ring3(j):
        m, _ = first[j % 2]
        n, at = second[j % 2]
        return (
            rs(j, 4, pbuf.at[j, m[0], n[2], 0:32], rs3.at[j, 0, 0:32], at(1)),
            rs(j, 5, pbuf.at[j, m[0], n[2], 32:64], rs3.at[j, 1, 0:32], at(3)),
        )

    def ring4(j):
        m, _ = first[j % 2]
        n, at = second[j % 2]
        return (
            rs(j, 6, pbuf.at[j, m[0], n[1]], rs4.at[j, 0], at(1)),
            rs(j, 7, pbuf.at[j, m[0], n[3]], rs4.at[j, 1], at(3)),
        )

    def ringed(j):
        return j // 2 < RINGED

    def spread(j):
        m, _ = first[j % 2]
        n, at = second[j % 2]
        return tuple(
            rs(j, 3 + d, pbuf.at[j, m[0], n[d]], rs3.at[j, d - 1], at(d)) for d in (1, 2, 3)
        )

    def final(j):
        slot, part = STEPS[j // 2]
        half = j % 2
        m, _ = first[half]
        n, _ = second[half]
        return remote(
            pbuf.at[j, m[0], n[0]], wfin.at[z, :, cols(half, part)], fs_sem.at[j], fr_sem.at[z, half, part],
            (last_seq, y_ids[SLOT_DY[slot]]),
        )

    def stage1(j):
        for copy in ring1(j):
            copy.start()

    def stage2(j):
        m, _ = first[j % 2]
        got, send = ring1(j), ring2(j)
        got[0].wait_recv()
        up = m[1]
        pbuf[j, up, 0:2] = pbuf[j, up, 0:2] + rs1[j, 0]
        send[0].start()
        got[1].wait_recv()
        down = m[3]
        pbuf[j, down, 2:4] = pbuf[j, down, 2:4] + rs1[j, 1]
        send[1].start()

    def stage3(j):
        m, _ = first[j % 2]
        for copy in ring2(j):
            copy.wait_recv()
        pbuf[j, m[0]] = pbuf[j, m[0]] + (rs2[j, 0] + rs2[j, 1])
        for copy in ring3(j) if ringed(j) else spread(j):
            copy.start()

    def stage4(j):
        m, _ = first[j % 2]
        n, _ = second[j % 2]
        got, send = ring3(j), ring4(j)
        got[0].wait_recv()
        pbuf[j, m[0], n[1], 0:32] = pbuf[j, m[0], n[1], 0:32] + rs3[j, 0, 0:32]
        send[0].start()
        got[1].wait_recv()
        pbuf[j, m[0], n[3], 32:64] = pbuf[j, m[0], n[3], 32:64] + rs3[j, 1, 0:32]
        send[1].start()

    def stage5(j):
        slot, part = STEPS[j // 2]
        half = j % 2
        m, _ = first[half]
        n, _ = second[half]
        if ringed(j):
            for copy in ring4(j):
                copy.wait_recv()
            pbuf[j, m[0], n[0]] = pbuf[j, m[0], n[0]] + (rs4[j, 0] + rs4[j, 1])
        else:
            for copy in spread(j):
                copy.wait_recv()
            pbuf[j, m[0], n[0]] = (pbuf[j, m[0], n[0]] + rs3[j, 0]) + (rs3[j, 1] + rs3[j, 2])
        if slot == 3:

            @pl.when(z != y)
            def _():
                final(j).start()

            @pl.when(z == y)
            def _():
                wfin[z, :, cols(half, part)] = pbuf[j, m[0], n[0]]
        else:
            final(j).start()

    stages = (stage1, stage2, stage3, stage4, stage5)

    def stage(k, p):
        for half in (0, 1):
            stages[k - 1](2 * p + half)

    def arrive(p, toks=(0, 1)):
        slot, part = STEPS[p]
        if slot == 3:
            if part == 0:
                x_own.wait()
        elif slot == 2:
            for tok in toks:
                for half in (0, 1):
                    x_forward(half, part, tok).wait_recv()
        else:
            x_direct(slot == 0, 1 - slot, part).wait_recv()

    lax.fori_loop(0, HEADS, rev_states, 0)
    send_a(0)
    lax.fori_loop(0, HEADS, fwd_states, 0)
    send_b(0)
    lax.fori_loop(0, HEADS * NCH, value_part, 0)
    send_c(0)
    send_a(1)
    other_parts(0, 2)
    recv_c(0)
    lax.fori_loop(0, HEADS, finish_values, 0)
    send_b(1)
    forward(0)
    lax.fori_loop(0, HEADS, take_values, 0)

    def step(p):
        arrive(p)
        product(p)
        stage(1, p)

    def finish(low, high):
        lax.fori_loop(low, high, finish_rest, 0)

    step(0)
    send_c(1)
    step(1)
    step(2)
    stage(2, 0)
    stage(2, 1)
    step(3)
    stage(3, 0)
    stage(2, 2)
    stage(3, 1)
    forward(1)
    other_parts(2, 3)
    stage(4, 0)
    stage(2, 3)
    stage(3, 2)
    stage(4, 1)
    other_parts(3, 4)
    stage(5, 0)
    stage(3, 3)
    stage(4, 2)
    stage(5, 1)
    step(4)
    stage(4, 3)
    stage(5, 2)
    step(5)
    stage(2, 4)
    stage(5, 3)
    recv_c(1)
    finish(0, 2)
    stage(2, 5)
    stage(3, 4)
    step(6)
    stage(3, 5)
    stage(4, 4)
    stage(2, 6)
    finish(2, 4)
    stage(4, 5)
    stage(5, 4)
    stage(3, 6)
    arrive(7, (0,))
    product(7, (0,))
    stage(5, 5)
    arrive(7, (1,))
    product(7, (1,))
    stage(1, 7)
    stage(5, 6)
    stage(2, 7)
    stage(3, 7)
    stage(5, 7)

    for part in range(4):
        for zs in range(4):

            @pl.when(jnp.logical_or(z != zs, z != y))
            def _(part=part, zs=zs):
                at = cols(part // 2, part % 2)
                sem = fr_sem.at[zs, part // 2, part % 2]
                remote(pbuf.at[0, 0, 0], wfin.at[zs, :, at], fs_sem.at[0], sem, sibling).wait_recv()

    w_out[...] = wfin[...].reshape(256, 512)

    for n in (0, 1):
        for h in range(HEADS):
            out_copy(n, h).wait()
    for st in (0, 1):
        for d in (1, 2, 3):
            ex_a(st, d).wait_send()
            ex_b(st, d).wait_send()
            ex_c(st, d).wait_send()
    for h in range(HEADS):
        vt_copy(h).wait_send()
    for half in (0, 1):
        for part in (0, 1):
            x_direct(True, half, part).wait_send()
            x_direct(False, half, part).wait_send()
            x_forward(half, part, 0).wait_send()
            x_forward(half, part, 1).wait_send()
    for j in range(JOBS):
        for ring in (ring1, ring2, ring3, ring4) if ringed(j) else (ring1, ring2, spread):
            for copy in ring(j):
                copy.wait_send()
        if STEPS[j // 2][0] == 3:

            @pl.when(z != y)
            def _(j=j):
                final(j).wait_send()
        else:
            final(j).wait_send()


def last_kernel(qg_in, kg_in, w_in, rowst, colst, qg_out, kg_out, upd, rown, coln, stage, wbuf, sem, w_sem):
    w_load = pltpu.make_async_copy(w_in, wbuf, w_sem)
    w_load.start()
    pieces = [(n, i) for n in (0, 1) for i in range(4)]

    def load(n, i):
        return pltpu.make_async_copy((qg_in, kg_in)[n].at[pl.ds(i * 256, 256)], stage.at[n, i], sem.at[0, n, i])

    def store(n, i):
        return pltpu.make_async_copy(stage.at[n, i], (qg_out, kg_out)[n].at[pl.ds(i * 256, 256)], sem.at[1, n, i])

    for piece in pieces:
        load(*piece).start()
    for piece in pieces:
        load(*piece).wait()
        store(*piece).start()
    w_load.wait()
    w = wbuf[...] / jnp.sqrt(F32(16384.0))
    squares = w * w + MOMENT_EPS
    row_mean = jnp.broadcast_to(jnp.mean(squares, axis=1, keepdims=True), (256, 128))
    col_mean = jnp.mean(squares, axis=0, keepdims=True)
    row_old = jnp.broadcast_to(rowst[...], (128, 256)).T
    row_new = DECAY * row_old + (1.0 - DECAY) * row_mean
    col_new = DECAY * colst[...] + (1.0 - DECAY) * col_mean
    rown[...] = row_new.T[0:1]
    coln[...] = col_new
    row_one = row_new[:, 0:1]
    average = jnp.mean(row_one, axis=0, keepdims=True)
    upd[...] = w * lax.rsqrt(row_one * col_new / average)
    for piece in pieces:
        store(*piece).wait()


def shards(queries, keys, values, out_grad, inputs, row_state, col_state):
    hbm = pl.BlockSpec(memory_space=pl.ANY)
    vmem = pl.BlockSpec(memory_space=pltpu.VMEM)
    dma = pltpu.SemaphoreType.DMA
    scratch = [
        pltpu.VMEM((4, HEADS, TOK, 128), F32),
        pltpu.VMEM((HEADS, TOK, 128), F32),
        pltpu.VMEM((HEADS, TOK, 128), F32),
        pltpu.VMEM((2 * HEADS, 128, TOK), F32),
        pltpu.VMEM((2 * HEADS, 128, 3 * TOK), BF16),
        pltpu.VMEM((4, TOK, 512), F32),
        pltpu.VMEM((3 * TOK, 2 * PART), BF16),
        pltpu.VMEM((HEADS, NCH, 128, 128), F32),
        pltpu.VMEM((HEADS, NCH, 128, 128), F32),
        pltpu.VMEM((2, HEADS, 128, 128), F32),
        pltpu.VMEM((2, 3, 128, 128), F32),
        pltpu.VMEM((2, 4, 128, 128), F32),
        pltpu.VMEM((2, 128, 128), F32),
        pltpu.VMEM((2, 3, 128, 128), F32),
        pltpu.VMEM((2, HEADS, 128, 128), F32),
        pltpu.VMEM((JOBS, 4, 4, 64, PART), F32),
        pltpu.VMEM((JOBS, 2, 2, 64, PART), F32),
        pltpu.VMEM((JOBS, 2, 4, 64, PART), F32),
        pltpu.VMEM((JOBS, 3, 64, PART), F32),
        pltpu.VMEM((JOBS, 2, 64, PART), F32),
        pltpu.VMEM((4, 64, 512), F32),
        dma((4, HEADS)),
        dma,
        dma((2, 2, 2)),
        dma((2, 2, 2)),
        dma((2, 4)),
        dma((2, 4)),
        dma((2, 3, 3)),
        dma((2, 3, 3)),
        dma((HEADS,)),
        dma((HEADS,)),
        dma((JOBS, 8)),
        dma((JOBS, 8)),
        dma((JOBS,)),
        dma((4, 2, 2)),
        dma((2, HEADS)),
    ]
    tokens = jax.ShapeDtypeStruct((TOK, 512), F32)
    block = jax.ShapeDtypeStruct((256, 512), F32)
    query_grad, key_grad, weight_grad = pl.pallas_call(
        kernel,
        out_shape=(tokens, tokens, block),
        in_specs=[hbm] * 5,
        out_specs=(hbm, hbm, vmem),
        scratch_shapes=scratch,
        compiler_params=pltpu.CompilerParams(
            collective_id=0, has_side_effects=True, vmem_limit_bytes=60 * 1024 * 1024
        ),
        cost_estimate=pl.CostEstimate(flops=20_000_000_000, bytes_accessed=16_000_000, transcendentals=0),
    )(queries, keys, values, out_grad, inputs)
    return pl.pallas_call(
        last_kernel,
        out_shape=(
            tokens,
            tokens,
            block,
            jax.ShapeDtypeStruct((1, 256), F32),
            jax.ShapeDtypeStruct((1, 512), F32),
        ),
        in_specs=[hbm] * 3 + [vmem] * 2,
        out_specs=(hbm, hbm, vmem, vmem, vmem),
        scratch_shapes=[pltpu.VMEM((2, 4, 256, 512), F32), pltpu.VMEM((256, 512), F32), dma((2, 2, 4)), dma],
        compiler_params=pltpu.CompilerParams(vmem_limit_bytes=60 * 1024 * 1024),
        cost_estimate=pl.CostEstimate(flops=2_000_000, bytes_accessed=10_000_000, transcendentals=131072),
    )(query_grad, key_grad, weight_grad, row_state, col_state)


def solution(mesh):
    in_specs = (
        P("seq", "head"),
        P("seq", "head"),
        P("seq", "head"),
        P("seq", "head"),
        P("seq", "head"),
        P("head", "seq"),
        P("seq", "head"),
    )
    out_specs = (
        P("seq", "head"),
        P("seq", "head"),
        P("seq", "head"),
        P("head", "seq"),
        P("seq", "head"),
    )
    return jax.shard_map(shards, mesh=mesh, in_specs=in_specs, out_specs=out_specs, check_vma=False)
```

```python
import jax
import jax.numpy as jnp
import numpy as np
from jax import lax
from jax.experimental import pallas as pl
from jax.experimental.pallas import tpu as pltpu
from jax.sharding import PartitionSpec as P

F32 = jnp.float32
BF16 = jnp.bfloat16
MESH = pl.DeviceIdType.MESH

HEAD_DIM = 128
TOK = 1024
HEADS = 4
CH = 256
NCH = TOK // CH
PART = 128
MOMENT_EPS = 1e-06
DECAY = 0.9
ATTN_SCALE = float(np.float32(1.0) / np.sqrt(np.float32(128 * 16384)))

NN = (((1,), (0,)), ((), ()))
NT = (((1,), (1,)), ((), ()))

SLOT_DY = (3, 1, 2, 0)
STEPS = ((3, 0), (3, 1), (0, 0), (1, 0), (0, 1), (1, 1), (2, 0), (2, 1))
JOBS = 2 * len(STEPS)
RINGED = 6


def dot(a, b, dims=NN):
    return lax.dot_general(a, b, dims, preferred_element_type=F32)


def split(a):
    hi = a.astype(BF16)
    lo = (a - hi.astype(F32)).astype(BF16)
    return hi, lo


def mm_nt(a, b):
    both = jnp.concatenate([a[0], a[1]], axis=1)
    twice = jnp.concatenate([b[0], b[0]], axis=1)
    return dot(both, twice, NT) + dot(a[0], b[1], NT)


def mm_nn(a, b):
    wide = jnp.concatenate([b[0], b[1]], axis=1)
    first = dot(a[0], wide)
    return first[:, :128] + first[:, 128:] + dot(a[1], b[0])


def mm_state(a, b):
    both = jnp.concatenate([a[0], a[1]], axis=1)
    wide = jnp.concatenate([b[0], b[1]], axis=1)
    out = dot(both, jnp.concatenate([wide, wide], axis=0))
    return out[:, :128] + out[:, 128:]


def mm3(a, b):
    return dot(a[0], b[0]) + dot(a[0], b[1]) + dot(a[1], b[0])


def kernel(
    q_hbm, k_hbm, v_hbm, g_hbm, x_hbm,
    qg_hbm, kg_hbm, w_out,
    io, qg, kg, vt, vtc, xbuf, xc,
    rev_c, fwd_c, tot, ex1, val, tz, ex2, enter,
    pbuf, rs1, rs2, rs3, rs4, wfin,
    ld_sem, xo_sem, xs_sem, xr_sem, xf_sem, xg_sem, es_sem, er_sem, vs_sem, vr_sem,
    rss_sem, rsr_sem, fs_sem, fr_sem, out_sem,
):
    sq = lax.axis_index("seq")
    hd = lax.axis_index("head")
    z, x = sq // 4, sq % 4
    y, c = hd // 2, hd % 2

    x_at = [x] + [(x + d) % 4 for d in (1, 2, 3)]
    z_at = [z] + [(z + d) % 4 for d in (1, 2, 3)]
    y_at = [y] + [(y + d) % 4 for d in (1, 2, 3)]
    x_ids = [z * 4 + x_at[d] for d in range(4)]
    z_ids = [z_at[d] * 4 + x for d in range(4)]
    y_ids = [y_at[d] * 2 + c for d in range(4)]
    last_seq = y * 4 + x

    def at_x(d):
        return (x_ids[d], hd)

    def at_z(d):
        return (z_ids[d], hd)

    def at_y(d):
        return (sq, y_ids[d])

    sibling = (sq, y * 2 + 1 - c)

    def remote(src, dst, send, recv, dev):
        return pltpu.make_async_remote_copy(
            src_ref=src, dst_ref=dst, send_sem=send, recv_sem=recv, device_id=dev, device_id_type=MESH
        )

    def load(n, h):
        src = (q_hbm, k_hbm, v_hbm, g_hbm)[n]
        return pltpu.make_async_copy(
            src.at[:, pl.ds(h * 128, 128)], io.at[n, h], ld_sem.at[n, h]
        )

    barrier = pltpu.get_barrier_semaphore()

    def greet(dev):
        pl.semaphore_signal(barrier, inc=1, device_id=dev, device_id_type=MESH)

    for dev in (at_y(1), at_y(3), sibling):
        greet(dev)
    for d in (1, 2, 3):
        greet(at_x(d))
        greet(at_z(d))
    for zs in range(4):

        @pl.when(jnp.logical_or(z != zs, z != y))
        def _(zs=zs):
            greet((zs * 4 + x, z * 2 + c))

    for n in (3, 0, 2, 1):
        for h in range(HEADS):
            load(n, h).start()

    pl.semaphore_wait(barrier, 12 + (z != y).astype(jnp.int32))

    def cols(half, part):
        return pl.ds(half * 256 + part * PART, PART)

    def x_direct(up, half, part):
        at = cols(half, part)
        slot = 0 if up else 1
        return remote(
            x_hbm.at[:, at], xbuf.at[slot, :, at], xs_sem.at[slot, half, part], xr_sem.at[slot, half, part],
            at_y(1 if up else 3),
        )

    def x_forward(half, part, tok):
        at = cols(half, part)
        span = pl.ds(tok * (TOK // 2), TOK // 2)
        sem = 2 * tok + part
        return remote(
            xbuf.at[half, span, at], xbuf.at[2, span, at], xf_sem.at[half, sem], xg_sem.at[half, sem],
            at_y(1 if half == 0 else 3),
        )

    def forward(part):
        x_direct(True, 0, part).wait_recv()
        x_direct(False, 1, part).wait_recv()
        for tok in (0, 1):
            x_forward(0, part, tok).start()
            x_forward(1, part, tok).start()

    for part in (0, 1):
        x_direct(True, 0, part).start()
        x_direct(False, 1, part).start()
        x_direct(True, 1, part).start()
        x_direct(False, 0, part).start()
    x_own = pltpu.make_async_copy(x_hbm, xbuf.at[3], xo_sem)
    x_own.start()

    def ex_a(st, d):
        dst = (x + d) % 4
        return remote(tot.at[st, dst], ex1.at[st, d - 1], es_sem.at[st, 0, d - 1], er_sem.at[st, 0, d - 1], at_x(d))

    def ex_b(st, d):
        return remote(tz.at[st], ex2.at[st, d - 1], es_sem.at[st, 1, d - 1], er_sem.at[st, 1, d - 1], at_z(d))

    def ex_c(st, d):
        return remote(val.at[st, d], enter.at[st, x], es_sem.at[st, 2, d - 1], er_sem.at[st, 2, d - 1], at_x(d))

    def counts(st, source, target):
        reached = source > target if st == 0 else source < target
        return reached.astype(F32)

    def send_a(st):
        for d in (1, 2, 3):
            ex_a(st, d).start()

    def send_b(st):
        for d in (1, 2, 3):
            ex_a(st, d).wait_recv()
        parts = [tot[st, x]] + [ex1[st, d - 1] for d in (1, 2, 3)]
        tz[st] = parts[0] + parts[1] + parts[2] + parts[3]
        for d in (1, 2, 3):
            ex_b(st, d).start()
        for e in range(4):
            target = (x + e) % 4
            terms = [counts(st, (x + 4 - d) % 4, target) * parts[d] for d in range(4)]
            val[st, e] = terms[0] + terms[1] + terms[2] + terms[3]

    def send_c(st):
        for d in (1, 2, 3):
            ex_b(st, d).wait_recv()
        base = sum(counts(st, (z + 4 - d) % 4, z) * ex2[st, d - 1] for d in (1, 2, 3))
        for e in (1, 2, 3):
            val[st, e] = val[st, e] + base
            ex_c(st, e).start()
        enter[st, x] = val[st, 0] + base

    def recv_c(st):
        for d in (1, 2, 3):
            remote(
                val.at[st, d], enter.at[st, (x + 4 - d) % 4],
                es_sem.at[st, 2, d - 1], er_sem.at[st, 2, d - 1], at_x(d),
            ).wait_recv()

    def rows(ch):
        return pl.ds(pl.multiple_of(ch * CH, CH), CH)

    def rev_states(h, carry):
        load(3, h).wait()
        load(0, h).wait()
        total = jnp.zeros((128, 128), F32)
        for ch in range(NCH):
            gt = split(io[3, h, ch * CH : (ch + 1) * CH].T)
            part = mm_nn(gt, split(io[0, h, ch * CH : (ch + 1) * CH]))
            rev_c[h, ch] = part
            total = total + part
        tot[0, h] = total
        return carry

    def fwd_states(h, carry):
        load(2, h).wait()
        load(1, h).wait()
        total = jnp.zeros((128, 128), F32)
        for ch in range(NCH):
            vtr = split(io[2, h, ch * CH : (ch + 1) * CH].T)
            part = mm_nn(vtr, split(io[1, h, ch * CH : (ch + 1) * CH]))
            fwd_c[h, ch] = part
            total = total + part
        tot[1, h] = total
        return carry

    row_at = lax.broadcasted_iota(jnp.int32, (CH, CH), 0)
    col_at = lax.broadcasted_iota(jnp.int32, (CH, CH), 1)

    causal = col_at <= row_at

    def value_part(i, carry):
        h, ch = i // NCH, i % NCH
        qk = mm_nt(split(io[0, h, rows(ch)]), split(io[1, h, rows(ch)]))
        vt[c * HEADS + h, :, rows(ch)] = mm3(split(io[3, h, rows(ch)].T), split(jnp.where(causal, qk, 0.0)))
        return carry

    def other_part(i, carry):
        h, ch = i // NCH, i % NCH
        q, k, v, g = (split(io[n, h, rows(ch)]) for n in range(4))
        gv = split(jnp.where(causal, mm_nt(g, v), 0.0))
        qg[h, rows(ch)] = mm_nn(gv, k)
        vg = split(jnp.where(row_at <= col_at, mm_nt(v, g), 0.0))
        kg[h, rows(ch)] = mm_nn(vg, q)
        return carry

    def other_parts(low, high):
        lax.fori_loop(low * NCH, high * NCH, other_part, 0)

    def vt_copy(h):
        at = c * HEADS + h
        return remote(vt.at[at], vt.at[at], vs_sem.at[h], vr_sem.at[h], sibling)

    def finish_values(h, carry):
        suffix = enter[0, h]
        at = c * HEADS + h
        for ch in reversed(range(NCH)):
            span = pl.ds(ch * CH, CH)
            more = mm_nt(split(suffix), split(io[1, h, span]))
            done = ATTN_SCALE * (vt[at, :, span] + more)
            vt[at, :, span] = done
            hi, lo = split(done)
            vtc[at, :, span] = hi
            vtc[at, :, pl.ds(TOK + ch * CH, CH)] = lo
            vtc[at, :, pl.ds(2 * TOK + ch * CH, CH)] = hi
            suffix = suffix + rev_c[h, ch]
        vt_copy(h).start()
        return carry


    def out_copy(n, h):
        dst = (qg_hbm, kg_hbm)[n]
        return pltpu.make_async_copy((qg, kg)[n].at[h], dst.at[:, pl.ds(h * 128, 128)], out_sem.at[n, h])

    def finish_keys(h):
        suffix = enter[0, h]
        for ch in reversed(range(NCH)):
            span = pl.ds(ch * CH, CH)
            kg[h, span] = ATTN_SCALE * (kg[h, span] + mm_state(split(io[2, h, span]), split(suffix)))
            suffix = suffix + rev_c[h, ch]

    def finish_queries(h):
        prefix = enter[1, h]
        for ch in range(NCH):
            span = pl.ds(ch * CH, CH)
            qg[h, span] = ATTN_SCALE * (qg[h, span] + mm_state(split(io[3, h, span]), split(prefix)))
            prefix = prefix + fwd_c[h, ch]

    def finish_rest(h, carry):
        finish_keys(h)
        finish_queries(h)
        out_copy(0, h).start()
        out_copy(1, h).start()
        return carry


    def take_values(h, carry):
        at = (1 - c) * HEADS + h
        remote(vt.at[at], vt.at[at], vs_sem.at[h], vr_sem.at[h], sibling).wait_recv()
        hi, lo = split(vt[at])
        vtc[at, :, 0:TOK] = hi
        vtc[at, :, TOK : 2 * TOK] = lo
        vtc[at, :, 2 * TOK : 3 * TOK] = hi
        return carry


    def product(p, toks=(0, 1)):
        slot, part = STEPS[p]

        def cut(t, carry):
            both = [xbuf[slot, rows(t), cols(half, part)] for half in (0, 1)]
            hi, lo = split(jnp.concatenate(both, axis=1))
            xc[rows(t)] = hi
            xc[rows(t + NCH)] = hi
            xc[rows(t + 2 * NCH)] = lo
            return carry

        lax.fori_loop(2 * toks[0], 2 * toks[-1] + 2, cut, 0)

        def block(a, carry):
            blocks = pl.ds(4 * a, 4)
            if len(toks) == 2:
                out = dot(vtc[blocks].reshape(512, 3 * TOK), xc[...])
            else:
                low = toks[0] * (TOK // 2)
                spans = [pl.ds(low + n * TOK, TOK // 2) for n in range(3)]
                out = sum(dot(vtc[blocks, :, span].reshape(512, TOK // 2), xc[span]) for span in spans)
            for b in (0, 1):
                near = out[b * 256 : (b + 1) * 256, :PART].reshape(4, 64, PART)
                at = 2 * a + b
                if toks[0] == 0:
                    pbuf[2 * p, at] = near
                else:
                    pbuf[2 * p, at] = pbuf[2 * p, at] + near
                for r in range(4):
                    far = out[b * 256 + r * 64 : b * 256 + (r + 1) * 64, PART:]
                    if toks[0] == 0:
                        pbuf[2 * p + 1, r, at] = far
                    else:
                        pbuf[2 * p + 1, r, at] = pbuf[2 * p + 1, r, at] + far
            return carry

        lax.fori_loop(0, 2, block, 0)

    first = ((x_at, at_x), (z_at, at_z))
    second = ((z_at, at_z), (x_at, at_x))

    def rs(j, n, src, dst, dev):
        return remote(src, dst, rss_sem.at[j, n], rsr_sem.at[j, n], dev)

    def ring1(j):
        m, at = first[j % 2]
        far = m[2]
        return (
            rs(j, 0, pbuf.at[j, far, 0:2], rs1.at[j, 0], at(1)),
            rs(j, 1, pbuf.at[j, far, 2:4], rs1.at[j, 1], at(3)),
        )

    def ring2(j):
        m, at = first[j % 2]
        return (
            rs(j, 2, pbuf.at[j, m[1]], rs2.at[j, 0], at(1)),
            rs(j, 3, pbuf.at[j, m[3]], rs2.at[j, 1], at(3)),
        )

    def ring3(j):
        m, _ = first[j % 2]
        n, at = second[j % 2]
        return (
            rs(j, 4, pbuf.at[j, m[0], n[2], 0:32], rs3.at[j, 0, 0:32], at(1)),
            rs(j, 5, pbuf.at[j, m[0], n[2], 32:64], rs3.at[j, 1, 0:32], at(3)),
        )

    def ring4(j):
        m, _ = first[j % 2]
        n, at = second[j % 2]
        return (
            rs(j, 6, pbuf.at[j, m[0], n[1]], rs4.at[j, 0], at(1)),
            rs(j, 7, pbuf.at[j, m[0], n[3]], rs4.at[j, 1], at(3)),
        )

    def ringed(j):
        return j // 2 < RINGED

    def spread(j):
        m, _ = first[j % 2]
        n, at = second[j % 2]
        return tuple(
            rs(j, 3 + d, pbuf.at[j, m[0], n[d]], rs3.at[j, d - 1], at(d)) for d in (1, 2, 3)
        )

    def final(j):
        slot, part = STEPS[j // 2]
        half = j % 2
        m, _ = first[half]
        n, _ = second[half]
        return remote(
            pbuf.at[j, m[0], n[0]], wfin.at[z, :, cols(half, part)], fs_sem.at[j], fr_sem.at[z, half, part],
            (last_seq, y_ids[SLOT_DY[slot]]),
        )

    def stage1(j):
        for copy in ring1(j):
            copy.start()

    def stage2(j):
        m, _ = first[j % 2]
        got, send = ring1(j), ring2(j)
        got[0].wait_recv()
        up = m[1]
        pbuf[j, up, 0:2] = pbuf[j, up, 0:2] + rs1[j, 0]
        send[0].start()
        got[1].wait_recv()
        down = m[3]
        pbuf[j, down, 2:4] = pbuf[j, down, 2:4] + rs1[j, 1]
        send[1].start()

    def stage3(j):
        m, _ = first[j % 2]
        for copy in ring2(j):
            copy.wait_recv()
        pbuf[j, m[0]] = pbuf[j, m[0]] + (rs2[j, 0] + rs2[j, 1])
        for copy in ring3(j) if ringed(j) else spread(j):
            copy.start()

    def stage4(j):
        m, _ = first[j % 2]
        n, _ = second[j % 2]
        got, send = ring3(j), ring4(j)
        got[0].wait_recv()
        pbuf[j, m[0], n[1], 0:32] = pbuf[j, m[0], n[1], 0:32] + rs3[j, 0, 0:32]
        send[0].start()
        got[1].wait_recv()
        pbuf[j, m[0], n[3], 32:64] = pbuf[j, m[0], n[3], 32:64] + rs3[j, 1, 0:32]
        send[1].start()

    def stage5(j):
        slot, part = STEPS[j // 2]
        half = j % 2
        m, _ = first[half]
        n, _ = second[half]
        if ringed(j):
            for copy in ring4(j):
                copy.wait_recv()
            pbuf[j, m[0], n[0]] = pbuf[j, m[0], n[0]] + (rs4[j, 0] + rs4[j, 1])
        else:
            for copy in spread(j):
                copy.wait_recv()
            pbuf[j, m[0], n[0]] = (pbuf[j, m[0], n[0]] + rs3[j, 0]) + (rs3[j, 1] + rs3[j, 2])
        if slot == 3:

            @pl.when(z != y)
            def _():
                final(j).start()

            @pl.when(z == y)
            def _():
                wfin[z, :, cols(half, part)] = pbuf[j, m[0], n[0]]
        else:
            final(j).start()

    stages = (stage1, stage2, stage3, stage4, stage5)

    def stage(k, p):
        for half in (0, 1):
            stages[k - 1](2 * p + half)

    def arrive(p, toks=(0, 1)):
        slot, part = STEPS[p]
        if slot == 3:
            if part == 0:
                x_own.wait()
        elif slot == 2:
            for tok in toks:
                for half in (0, 1):
                    x_forward(half, part, tok).wait_recv()
        else:
            x_direct(slot == 0, 1 - slot, part).wait_recv()

    lax.fori_loop(0, HEADS, rev_states, 0)
    send_a(0)
    lax.fori_loop(0, HEADS, fwd_states, 0)
    send_b(0)
    lax.fori_loop(0, HEADS * NCH, value_part, 0)
    send_c(0)
    send_a(1)
    other_parts(0, 2)
    recv_c(0)
    lax.fori_loop(0, HEADS, finish_values, 0)
    send_b(1)
    forward(0)
    lax.fori_loop(0, HEADS, take_values, 0)

    def step(p):
        arrive(p)
        product(p)
        stage(1, p)

    def finish(low, high):
        lax.fori_loop(low, high, finish_rest, 0)

    step(0)
    send_c(1)
    step(1)
    stage(2, 0)
    step(2)
    stage(2, 1)
    stage(3, 0)
    step(3)
    stage(2, 2)
    stage(3, 1)
    stage(4, 0)
    forward(1)
    other_parts(2, 3)
    stage(2, 3)
    stage(3, 2)
    stage(4, 1)
    stage(5, 0)
    other_parts(3, 4)
    stage(3, 3)
    stage(4, 2)
    stage(5, 1)
    step(4)
    stage(4, 3)
    stage(5, 2)
    step(5)
    stage(2, 4)
    stage(5, 3)
    recv_c(1)
    finish(0, 2)
    stage(2, 5)
    stage(3, 4)
    step(6)
    stage(3, 5)
    stage(4, 4)
    stage(2, 6)
    finish(2, 4)
    stage(4, 5)
    stage(5, 4)
    stage(3, 6)
    arrive(7, (0,))
    product(7, (0,))
    stage(5, 5)
    arrive(7, (1,))
    product(7, (1,))
    stage(1, 7)
    stage(5, 6)
    stage(2, 7)
    stage(3, 7)
    stage(5, 7)

    for part in range(4):
        for zs in range(4):

            @pl.when(jnp.logical_or(z != zs, z != y))
            def _(part=part, zs=zs):
                at = cols(part // 2, part % 2)
                sem = fr_sem.at[zs, part // 2, part % 2]
                remote(pbuf.at[0, 0, 0], wfin.at[zs, :, at], fs_sem.at[0], sem, sibling).wait_recv()

    w_out[...] = wfin[...].reshape(256, 512)

    for n in (0, 1):
        for h in range(HEADS):
            out_copy(n, h).wait()
    for st in (0, 1):
        for d in (1, 2, 3):
            ex_a(st, d).wait_send()
            ex_b(st, d).wait_send()
            ex_c(st, d).wait_send()
    for h in range(HEADS):
        vt_copy(h).wait_send()
    for half in (0, 1):
        for part in (0, 1):
            x_direct(True, half, part).wait_send()
            x_direct(False, half, part).wait_send()
            x_forward(half, part, 0).wait_send()
            x_forward(half, part, 1).wait_send()
    for j in range(JOBS):
        for ring in (ring1, ring2, ring3, ring4) if ringed(j) else (ring1, ring2, spread):
            for copy in ring(j):
                copy.wait_send()
        if STEPS[j // 2][0] == 3:

            @pl.when(z != y)
            def _(j=j):
                final(j).wait_send()
        else:
            final(j).wait_send()


def last_kernel(qg_in, kg_in, w_in, rowst, colst, qg_out, kg_out, upd, rown, coln, stage, wbuf, sem, w_sem):
    w_load = pltpu.make_async_copy(w_in, wbuf, w_sem)
    w_load.start()
    pieces = [(n, i) for n in (0, 1) for i in range(4)]

    def load(n, i):
        return pltpu.make_async_copy((qg_in, kg_in)[n].at[pl.ds(i * 256, 256)], stage.at[n, i], sem.at[0, n, i])

    def store(n, i):
        return pltpu.make_async_copy(stage.at[n, i], (qg_out, kg_out)[n].at[pl.ds(i * 256, 256)], sem.at[1, n, i])

    for piece in pieces:
        load(*piece).start()
    for piece in pieces[:4]:
        load(*piece).wait()
        store(*piece).start()
    w_load.wait()
    w = wbuf[...] / jnp.sqrt(F32(16384.0))
    squares = w * w + MOMENT_EPS
    row_mean = jnp.broadcast_to(jnp.mean(squares, axis=1, keepdims=True), (256, 128))
    col_mean = jnp.mean(squares, axis=0, keepdims=True)
    row_old = jnp.broadcast_to(rowst[...], (128, 256)).T
    row_new = DECAY * row_old + (1.0 - DECAY) * row_mean
    col_new = DECAY * colst[...] + (1.0 - DECAY) * col_mean
    rown[...] = row_new.T[0:1]
    coln[...] = col_new
    row_one = row_new[:, 0:1]
    average = jnp.mean(row_one, axis=0, keepdims=True)
    for piece in pieces[4:]:
        load(*piece).wait()
        store(*piece).start()
    upd[...] = w * lax.rsqrt(row_one * col_new / average)
    for piece in pieces:
        store(*piece).wait()


def shards(queries, keys, values, out_grad, inputs, row_state, col_state):
    hbm = pl.BlockSpec(memory_space=pl.ANY)
    vmem = pl.BlockSpec(memory_space=pltpu.VMEM)
    dma = pltpu.SemaphoreType.DMA
    scratch = [
        pltpu.VMEM((4, HEADS, TOK, 128), F32),
        pltpu.VMEM((HEADS, TOK, 128), F32),
        pltpu.VMEM((HEADS, TOK, 128), F32),
        pltpu.VMEM((2 * HEADS, 128, TOK), F32),
        pltpu.VMEM((2 * HEADS, 128, 3 * TOK), BF16),
        pltpu.VMEM((4, TOK, 512), F32),
        pltpu.VMEM((3 * TOK, 2 * PART), BF16),
        pltpu.VMEM((HEADS, NCH, 128, 128), F32),
        pltpu.VMEM((HEADS, NCH, 128, 128), F32),
        pltpu.VMEM((2, HEADS, 128, 128), F32),
        pltpu.VMEM((2, 3, 128, 128), F32),
        pltpu.VMEM((2, 4, 128, 128), F32),
        pltpu.VMEM((2, 128, 128), F32),
        pltpu.VMEM((2, 3, 128, 128), F32),
        pltpu.VMEM((2, HEADS, 128, 128), F32),
        pltpu.VMEM((JOBS, 4, 4, 64, PART), F32),
        pltpu.VMEM((JOBS, 2, 2, 64, PART), F32),
        pltpu.VMEM((JOBS, 2, 4, 64, PART), F32),
        pltpu.VMEM((JOBS, 3, 64, PART), F32),
        pltpu.VMEM((JOBS, 2, 64, PART), F32),
        pltpu.VMEM((4, 64, 512), F32),
        dma((4, HEADS)),
        dma,
        dma((2, 2, 2)),
        dma((2, 2, 2)),
        dma((2, 4)),
        dma((2, 4)),
        dma((2, 3, 3)),
        dma((2, 3, 3)),
        dma((HEADS,)),
        dma((HEADS,)),
        dma((JOBS, 8)),
        dma((JOBS, 8)),
        dma((JOBS,)),
        dma((4, 2, 2)),
        dma((2, HEADS)),
    ]
    tokens = jax.ShapeDtypeStruct((TOK, 512), F32)
    block = jax.ShapeDtypeStruct((256, 512), F32)
    query_grad, key_grad, weight_grad = pl.pallas_call(
        kernel,
        out_shape=(tokens, tokens, block),
        in_specs=[hbm] * 5,
        out_specs=(hbm, hbm, vmem),
        scratch_shapes=scratch,
        compiler_params=pltpu.CompilerParams(
            collective_id=0, has_side_effects=True, vmem_limit_bytes=60 * 1024 * 1024
        ),
        cost_estimate=pl.CostEstimate(flops=20_000_000_000, bytes_accessed=16_000_000, transcendentals=0),
    )(queries, keys, values, out_grad, inputs)
    return pl.pallas_call(
        last_kernel,
        out_shape=(
            tokens,
            tokens,
            block,
            jax.ShapeDtypeStruct((1, 256), F32),
            jax.ShapeDtypeStruct((1, 512), F32),
        ),
        in_specs=[hbm] * 3 + [vmem] * 2,
        out_specs=(hbm, hbm, vmem, vmem, vmem),
        scratch_shapes=[pltpu.VMEM((2, 4, 256, 512), F32), pltpu.VMEM((256, 512), F32), dma((2, 2, 4)), dma],
        compiler_params=pltpu.CompilerParams(vmem_limit_bytes=60 * 1024 * 1024),
        cost_estimate=pl.CostEstimate(flops=2_000_000, bytes_accessed=10_000_000, transcendentals=131072),
    )(query_grad, key_grad, weight_grad, row_state, col_state)


def solution(mesh):
    in_specs = (
        P("seq", "head"),
        P("seq", "head"),
        P("seq", "head"),
        P("seq", "head"),
        P("seq", "head"),
        P("head", "seq"),
        P("seq", "head"),
    )
    out_specs = (
        P("seq", "head"),
        P("seq", "head"),
        P("seq", "head"),
        P("head", "seq"),
        P("seq", "head"),
    )
    return jax.shard_map(shards, mesh=mesh, in_specs=in_specs, out_specs=out_specs, check_vma=False)
```

```python
import jax
import jax.numpy as jnp
import numpy as np
from jax import lax
from jax.experimental import pallas as pl
from jax.experimental.pallas import tpu as pltpu
from jax.sharding import PartitionSpec as P

F32 = jnp.float32
BF16 = jnp.bfloat16
MESH = pl.DeviceIdType.MESH

HEAD_DIM = 128
TOK = 1024
HEADS = 4
CH = 256
NCH = TOK // CH
PART = 128
MOMENT_EPS = 1e-06
DECAY = 0.9
ATTN_SCALE = float(np.float32(1.0) / np.sqrt(np.float32(128 * 16384)))

NN = (((1,), (0,)), ((), ()))
NT = (((1,), (1,)), ((), ()))

SLOT_DY = (3, 1, 2, 0)
STEPS = ((3, 0), (3, 1), (0, 0), (1, 0), (0, 1), (1, 1), (2, 0), (2, 1))
JOBS = 2 * len(STEPS)
RINGED = 6


def dot(a, b, dims=NN):
    return lax.dot_general(a, b, dims, preferred_element_type=F32)


def split(a):
    hi = a.astype(BF16)
    lo = (a - hi.astype(F32)).astype(BF16)
    return hi, lo


def mm_nt(a, b):
    both = jnp.concatenate([a[0], a[1]], axis=1)
    twice = jnp.concatenate([b[0], b[0]], axis=1)
    return dot(both, twice, NT) + dot(a[0], b[1], NT)


def mm_nn(a, b):
    wide = jnp.concatenate([b[0], b[1]], axis=1)
    first = dot(a[0], wide)
    return first[:, :128] + first[:, 128:] + dot(a[1], b[0])


def mm_state(a, b):
    both = jnp.concatenate([a[0], a[1]], axis=1)
    wide = jnp.concatenate([b[0], b[1]], axis=1)
    out = dot(both, jnp.concatenate([wide, wide], axis=0))
    return out[:, :128] + out[:, 128:]


def mm3(a, b):
    return dot(a[0], b[0]) + dot(a[0], b[1]) + dot(a[1], b[0])


def kernel(
    q_hbm, k_hbm, v_hbm, g_hbm, x_hbm,
    qg_hbm, kg_hbm, w_out,
    io, qg, kg, vt, vtc, xbuf, xc,
    rev_c, fwd_c, tot, ex1, val, tz, ex2, enter,
    pbuf, rs1, rs2, rs3, rs4, wfin,
    ld_sem, xo_sem, xs_sem, xr_sem, xf_sem, xg_sem, es_sem, er_sem, vs_sem, vr_sem,
    rss_sem, rsr_sem, fs_sem, fr_sem, out_sem,
):
    sq = lax.axis_index("seq")
    hd = lax.axis_index("head")
    z, x = sq // 4, sq % 4
    y, c = hd // 2, hd % 2

    x_at = [x] + [(x + d) % 4 for d in (1, 2, 3)]
    z_at = [z] + [(z + d) % 4 for d in (1, 2, 3)]
    y_at = [y] + [(y + d) % 4 for d in (1, 2, 3)]
    x_ids = [z * 4 + x_at[d] for d in range(4)]
    z_ids = [z_at[d] * 4 + x for d in range(4)]
    y_ids = [y_at[d] * 2 + c for d in range(4)]
    last_seq = y * 4 + x

    def at_x(d):
        return (x_ids[d], hd)

    def at_z(d):
        return (z_ids[d], hd)

    def at_y(d):
        return (sq, y_ids[d])

    sibling = (sq, y * 2 + 1 - c)

    def remote(src, dst, send, recv, dev):
        return pltpu.make_async_remote_copy(
            src_ref=src, dst_ref=dst, send_sem=send, recv_sem=recv, device_id=dev, device_id_type=MESH
        )

    def load(n, h):
        src = (q_hbm, k_hbm, v_hbm, g_hbm)[n]
        return pltpu.make_async_copy(
            src.at[:, pl.ds(h * 128, 128)], io.at[n, h], ld_sem.at[n, h]
        )

    barrier = pltpu.get_barrier_semaphore()

    def greet(dev):
        pl.semaphore_signal(barrier, inc=1, device_id=dev, device_id_type=MESH)

    for dev in (at_y(1), at_y(3), sibling):
        greet(dev)
    for d in (1, 2, 3):
        greet(at_x(d))
        greet(at_z(d))
    for zs in range(4):

        @pl.when(jnp.logical_or(z != zs, z != y))
        def _(zs=zs):
            greet((zs * 4 + x, z * 2 + c))

    for n in (3, 0, 2, 1):
        for h in range(HEADS):
            load(n, h).start()

    pl.semaphore_wait(barrier, 12 + (z != y).astype(jnp.int32))

    def cols(half, part):
        return pl.ds(half * 256 + part * PART, PART)

    def x_direct(up, half, part):
        at = cols(half, part)
        slot = 0 if up else 1
        return remote(
            x_hbm.at[:, at], xbuf.at[slot, :, at], xs_sem.at[slot, half, part], xr_sem.at[slot, half, part],
            at_y(1 if up else 3),
        )

    def x_forward(half, part, tok):
        at = cols(half, part)
        span = pl.ds(tok * (TOK // 2), TOK // 2)
        sem = 2 * tok + part
        return remote(
            xbuf.at[half, span, at], xbuf.at[2, span, at], xf_sem.at[half, sem], xg_sem.at[half, sem],
            at_y(1 if half == 0 else 3),
        )

    def forward(part):
        x_direct(True, 0, part).wait_recv()
        x_direct(False, 1, part).wait_recv()
        for tok in (0, 1):
            x_forward(0, part, tok).start()
            x_forward(1, part, tok).start()

    for part in (0, 1):
        x_direct(True, 0, part).start()
        x_direct(False, 1, part).start()
        x_direct(True, 1, part).start()
        x_direct(False, 0, part).start()
    x_own = pltpu.make_async_copy(x_hbm, xbuf.at[3], xo_sem)
    x_own.start()

    def ex_a(st, d):
        dst = (x + d) % 4
        return remote(tot.at[st, dst], ex1.at[st, d - 1], es_sem.at[st, 0, d - 1], er_sem.at[st, 0, d - 1], at_x(d))

    def ex_b(st, d):
        return remote(tz.at[st], ex2.at[st, d - 1], es_sem.at[st, 1, d - 1], er_sem.at[st, 1, d - 1], at_z(d))

    def ex_c(st, d):
        return remote(val.at[st, d], enter.at[st, x], es_sem.at[st, 2, d - 1], er_sem.at[st, 2, d - 1], at_x(d))

    def counts(st, source, target):
        reached = source > target if st == 0 else source < target
        return reached.astype(F32)

    def send_a(st):
        for d in (2, 1, 3):
            ex_a(st, d).start()

    def send_b(st):
        for d in (1, 2, 3):
            ex_a(st, d).wait_recv()
        parts = [tot[st, x]] + [ex1[st, d - 1] for d in (1, 2, 3)]
        tz[st] = parts[0] + parts[1] + parts[2] + parts[3]
        for d in (2, 1, 3):
            ex_b(st, d).start()
        for e in range(4):
            target = (x + e) % 4
            terms = [counts(st, (x + 4 - d) % 4, target) * parts[d] for d in range(4)]
            val[st, e] = terms[0] + terms[1] + terms[2] + terms[3]

    def send_c(st):
        for d in (1, 2, 3):
            ex_b(st, d).wait_recv()
        base = sum(counts(st, (z + 4 - d) % 4, z) * ex2[st, d - 1] for d in (1, 2, 3))
        for e in (2, 1, 3):
            val[st, e] = val[st, e] + base
            ex_c(st, e).start()
        enter[st, x] = val[st, 0] + base

    def recv_c(st):
        for d in (1, 2, 3):
            remote(
                val.at[st, d], enter.at[st, (x + 4 - d) % 4],
                es_sem.at[st, 2, d - 1], er_sem.at[st, 2, d - 1], at_x(d),
            ).wait_recv()

    def rows(ch):
        return pl.ds(pl.multiple_of(ch * CH, CH), CH)

    def rev_states(h, carry):
        load(3, h).wait()
        load(0, h).wait()
        total = jnp.zeros((128, 128), F32)
        for ch in range(NCH):
            gt = split(io[3, h, ch * CH : (ch + 1) * CH].T)
            part = mm_nn(gt, split(io[0, h, ch * CH : (ch + 1) * CH]))
            rev_c[h, ch] = part
            total = total + part
        tot[0, h] = total
        return carry

    def fwd_states(h, carry):
        load(2, h).wait()
        load(1, h).wait()
        total = jnp.zeros((128, 128), F32)
        for ch in range(NCH):
            vtr = split(io[2, h, ch * CH : (ch + 1) * CH].T)
            part = mm_nn(vtr, split(io[1, h, ch * CH : (ch + 1) * CH]))
            fwd_c[h, ch] = part
            total = total + part
        tot[1, h] = total
        return carry

    row_at = lax.broadcasted_iota(jnp.int32, (CH, CH), 0)
    col_at = lax.broadcasted_iota(jnp.int32, (CH, CH), 1)

    causal = col_at <= row_at

    def value_part(i, carry):
        h, ch = i // NCH, i % NCH
        qk = mm_nt(split(io[0, h, rows(ch)]), split(io[1, h, rows(ch)]))
        vt[c * HEADS + h, :, rows(ch)] = mm3(split(io[3, h, rows(ch)].T), split(jnp.where(causal, qk, 0.0)))
        return carry

    def other_part(i, carry):
        h, ch = i // NCH, i % NCH
        q, k, v, g = (split(io[n, h, rows(ch)]) for n in range(4))
        gv = split(jnp.where(causal, mm_nt(g, v), 0.0))
        qg[h, rows(ch)] = mm_nn(gv, k)
        vg = split(jnp.where(row_at <= col_at, mm_nt(v, g), 0.0))
        kg[h, rows(ch)] = mm_nn(vg, q)
        return carry

    def other_parts(low, high):
        lax.fori_loop(low * NCH, high * NCH, other_part, 0)

    def vt_copy(h):
        at = c * HEADS + h
        return remote(vt.at[at], vt.at[at], vs_sem.at[h], vr_sem.at[h], sibling)

    def finish_values(h, carry):
        suffix = enter[0, h]
        at = c * HEADS + h
        for ch in reversed(range(NCH)):
            span = pl.ds(ch * CH, CH)
            more = mm_nt(split(suffix), split(io[1, h, span]))
            done = ATTN_SCALE * (vt[at, :, span] + more)
            vt[at, :, span] = done
            hi, lo = split(done)
            vtc[at, :, span] = hi
            vtc[at, :, pl.ds(TOK + ch * CH, CH)] = lo
            vtc[at, :, pl.ds(2 * TOK + ch * CH, CH)] = hi
            suffix = suffix + rev_c[h, ch]
        vt_copy(h).start()
        return carry


    def out_copy(n, h):
        dst = (qg_hbm, kg_hbm)[n]
        return pltpu.make_async_copy((qg, kg)[n].at[h], dst.at[:, pl.ds(h * 128, 128)], out_sem.at[n, h])

    def finish_keys(h):
        suffix = enter[0, h]
        for ch in reversed(range(NCH)):
            span = pl.ds(ch * CH, CH)
            kg[h, span] = ATTN_SCALE * (kg[h, span] + mm_state(split(io[2, h, span]), split(suffix)))
            suffix = suffix + rev_c[h, ch]

    def finish_queries(h):
        prefix = enter[1, h]
        for ch in range(NCH):
            span = pl.ds(ch * CH, CH)
            qg[h, span] = ATTN_SCALE * (qg[h, span] + mm_state(split(io[3, h, span]), split(prefix)))
            prefix = prefix + fwd_c[h, ch]

    def finish_rest(h, carry):
        finish_keys(h)
        finish_queries(h)
        out_copy(0, h).start()
        out_copy(1, h).start()
        return carry


    def take_values(h, carry):
        at = (1 - c) * HEADS + h
        remote(vt.at[at], vt.at[at], vs_sem.at[h], vr_sem.at[h], sibling).wait_recv()
        hi, lo = split(vt[at])
        vtc[at, :, 0:TOK] = hi
        vtc[at, :, TOK : 2 * TOK] = lo
        vtc[at, :, 2 * TOK : 3 * TOK] = hi
        return carry


    def product(p, toks=(0, 1), between=None):
        slot, part = STEPS[p]

        def cut(t, carry):
            both = [xbuf[slot, rows(t), cols(half, part)] for half in (0, 1)]
            hi, lo = split(jnp.concatenate(both, axis=1))
            xc[rows(t)] = hi
            xc[rows(t + NCH)] = hi
            xc[rows(t + 2 * NCH)] = lo
            return carry

        lax.fori_loop(2 * toks[0], 2 * toks[-1] + 2, cut, 0)

        def block(a, carry):
            blocks = pl.ds(4 * a, 4)
            if len(toks) == 2:
                out = dot(vtc[blocks].reshape(512, 3 * TOK), xc[...])
            else:
                low = toks[0] * (TOK // 2)
                spans = [pl.ds(low + n * TOK, TOK // 2) for n in range(3)]
                out = sum(dot(vtc[blocks, :, span].reshape(512, TOK // 2), xc[span]) for span in spans)
            for b in (0, 1):
                near = out[b * 256 : (b + 1) * 256, :PART].reshape(4, 64, PART)
                at = 2 * a + b
                if toks[0] == 0:
                    pbuf[2 * p, at] = near
                else:
                    pbuf[2 * p, at] = pbuf[2 * p, at] + near
                for r in range(4):
                    far = out[b * 256 + r * 64 : b * 256 + (r + 1) * 64, PART:]
                    if toks[0] == 0:
                        pbuf[2 * p + 1, r, at] = far
                    else:
                        pbuf[2 * p + 1, r, at] = pbuf[2 * p + 1, r, at] + far
            return carry

        if between is None:
            lax.fori_loop(0, 2, block, 0)
        else:
            block(c, 0)
            between()
            block(1 - c, 0)

    first = ((x_at, at_x), (z_at, at_z))
    second = ((z_at, at_z), (x_at, at_x))

    def rs(j, n, src, dst, dev):
        return remote(src, dst, rss_sem.at[j, n], rsr_sem.at[j, n], dev)

    def ring1(j):
        m, at = first[j % 2]
        far = m[2]
        return (
            rs(j, 0, pbuf.at[j, far, 0:2], rs1.at[j, 0], at(1)),
            rs(j, 1, pbuf.at[j, far, 2:4], rs1.at[j, 1], at(3)),
        )

    def ring2(j):
        m, at = first[j % 2]
        return (
            rs(j, 2, pbuf.at[j, m[1]], rs2.at[j, 0], at(1)),
            rs(j, 3, pbuf.at[j, m[3]], rs2.at[j, 1], at(3)),
        )

    def ring3(j):
        m, _ = first[j % 2]
        n, at = second[j % 2]
        return (
            rs(j, 4, pbuf.at[j, m[0], n[2], 0:32], rs3.at[j, 0, 0:32], at(1)),
            rs(j, 5, pbuf.at[j, m[0], n[2], 32:64], rs3.at[j, 1, 0:32], at(3)),
        )

    def ring4(j):
        m, _ = first[j % 2]
        n, at = second[j % 2]
        return (
            rs(j, 6, pbuf.at[j, m[0], n[1]], rs4.at[j, 0], at(1)),
            rs(j, 7, pbuf.at[j, m[0], n[3]], rs4.at[j, 1], at(3)),
        )

    def ringed(j):
        return j // 2 < RINGED

    def spread(j):
        m, _ = first[j % 2]
        n, at = second[j % 2]
        return tuple(
            rs(j, 3 + d, pbuf.at[j, m[0], n[d]], rs3.at[j, d - 1], at(d)) for d in (1, 2, 3)
        )

    def final(j):
        slot, part = STEPS[j // 2]
        half = j % 2
        m, _ = first[half]
        n, _ = second[half]
        return remote(
            pbuf.at[j, m[0], n[0]], wfin.at[z, :, cols(half, part)], fs_sem.at[j], fr_sem.at[z, half, part],
            (last_seq, y_ids[SLOT_DY[slot]]),
        )

    def stage1(j):
        for copy in ring1(j):
            copy.start()

    def stage2(j):
        m, _ = first[j % 2]
        got, send = ring1(j), ring2(j)
        got[0].wait_recv()
        up = m[1]
        pbuf[j, up, 0:2] = pbuf[j, up, 0:2] + rs1[j, 0]
        send[0].start()
        got[1].wait_recv()
        down = m[3]
        pbuf[j, down, 2:4] = pbuf[j, down, 2:4] + rs1[j, 1]
        send[1].start()

    def stage3(j):
        m, _ = first[j % 2]
        for copy in ring2(j):
            copy.wait_recv()
        pbuf[j, m[0]] = pbuf[j, m[0]] + (rs2[j, 0] + rs2[j, 1])
        for copy in ring3(j) if ringed(j) else spread(j):
            copy.start()

    def stage4(j):
        m, _ = first[j % 2]
        n, _ = second[j % 2]
        got, send = ring3(j), ring4(j)
        got[0].wait_recv()
        pbuf[j, m[0], n[1], 0:32] = pbuf[j, m[0], n[1], 0:32] + rs3[j, 0, 0:32]
        send[0].start()
        got[1].wait_recv()
        pbuf[j, m[0], n[3], 32:64] = pbuf[j, m[0], n[3], 32:64] + rs3[j, 1, 0:32]
        send[1].start()

    def stage5(j):
        slot, part = STEPS[j // 2]
        half = j % 2
        m, _ = first[half]
        n, _ = second[half]
        if ringed(j):
            for copy in ring4(j):
                copy.wait_recv()
            pbuf[j, m[0], n[0]] = pbuf[j, m[0], n[0]] + (rs4[j, 0] + rs4[j, 1])
        else:
            for copy in spread(j):
                copy.wait_recv()
            pbuf[j, m[0], n[0]] = (pbuf[j, m[0], n[0]] + rs3[j, 0]) + (rs3[j, 1] + rs3[j, 2])
        if slot == 3:

            @pl.when(z != y)
            def _():
                final(j).start()

            @pl.when(z == y)
            def _():
                wfin[z, :, cols(half, part)] = pbuf[j, m[0], n[0]]
        else:
            final(j).start()

    stages = (stage1, stage2, stage3, stage4, stage5)

    def stage(k, p):
        for half in (0, 1):
            stages[k - 1](2 * p + half)

    def arrive(p, toks=(0, 1)):
        slot, part = STEPS[p]
        if slot == 3:
            if part == 0:
                x_own.wait()
        elif slot == 2:
            for tok in toks:
                for half in (0, 1):
                    x_forward(half, part, tok).wait_recv()
        else:
            x_direct(slot == 0, 1 - slot, part).wait_recv()

    lax.fori_loop(0, HEADS, rev_states, 0)
    send_a(0)
    lax.fori_loop(0, HEADS, fwd_states, 0)
    send_b(0)
    lax.fori_loop(0, HEADS * NCH, value_part, 0)
    send_c(0)
    send_a(1)
    other_parts(0, 2)
    recv_c(0)
    lax.fori_loop(0, HEADS, finish_values, 0)
    send_b(1)
    forward(0)

    def step(p):
        arrive(p)
        product(p)
        stage(1, p)

    def finish(low, high):
        lax.fori_loop(low, high, finish_rest, 0)

    arrive(0)
    product(0, between=lambda: lax.fori_loop(0, HEADS, take_values, 0))
    stage(1, 0)
    send_c(1)
    step(1)
    stage(2, 0)
    step(2)
    stage(2, 1)
    stage(3, 0)
    step(3)
    stage(2, 2)
    stage(3, 1)
    stage(4, 0)
    forward(1)
    other_parts(2, 3)
    stage(2, 3)
    stage(3, 2)
    stage(4, 1)
    stage(5, 0)
    other_parts(3, 4)
    stage(3, 3)
    stage(4, 2)
    stage(5, 1)
    step(4)
    stage(4, 3)
    stage(5, 2)
    step(5)
    stage(2, 4)
    stage(5, 3)
    recv_c(1)
    finish(0, 2)
    stage(2, 5)
    stage(3, 4)
    step(6)
    stage(3, 5)
    stage(4, 4)
    stage(2, 6)
    finish(2, 4)
    stage(4, 5)
    stage(5, 4)
    stage(3, 6)
    arrive(7, (0,))
    product(7, (0,))
    stage(5, 5)
    arrive(7, (1,))
    product(7, (1,))
    stage(1, 7)
    stage(5, 6)
    stage(2, 7)
    stage(3, 7)
    stage(5, 7)

    for part in range(4):
        for zs in range(4):

            @pl.when(jnp.logical_or(z != zs, z != y))
            def _(part=part, zs=zs):
                at = cols(part // 2, part % 2)
                sem = fr_sem.at[zs, part // 2, part % 2]
                remote(pbuf.at[0, 0, 0], wfin.at[zs, :, at], fs_sem.at[0], sem, sibling).wait_recv()

    w_out[...] = wfin[...].reshape(256, 512)

    for n in (0, 1):
        for h in range(HEADS):
            out_copy(n, h).wait()
    for st in (0, 1):
        for d in (1, 2, 3):
            ex_a(st, d).wait_send()
            ex_b(st, d).wait_send()
            ex_c(st, d).wait_send()
    for h in range(HEADS):
        vt_copy(h).wait_send()
    for half in (0, 1):
        for part in (0, 1):
            x_direct(True, half, part).wait_send()
            x_direct(False, half, part).wait_send()
            x_forward(half, part, 0).wait_send()
            x_forward(half, part, 1).wait_send()
    for j in range(JOBS):
        for ring in (ring1, ring2, ring3, ring4) if ringed(j) else (ring1, ring2, spread):
            for copy in ring(j):
                copy.wait_send()
        if STEPS[j // 2][0] == 3:

            @pl.when(z != y)
            def _(j=j):
                final(j).wait_send()
        else:
            final(j).wait_send()


def last_kernel(qg_in, kg_in, w_in, rowst, colst, qg_out, kg_out, upd, rown, coln, stage, wbuf, sem, w_sem):
    w_load = pltpu.make_async_copy(w_in, wbuf, w_sem)
    w_load.start()
    pieces = [(n, i) for n in (0, 1) for i in range(4)]

    def load(n, i):
        return pltpu.make_async_copy((qg_in, kg_in)[n].at[pl.ds(i * 256, 256)], stage.at[n, i], sem.at[0, n, i])

    def store(n, i):
        return pltpu.make_async_copy(stage.at[n, i], (qg_out, kg_out)[n].at[pl.ds(i * 256, 256)], sem.at[1, n, i])

    for piece in pieces:
        load(*piece).start()
    for piece in pieces:
        load(*piece).wait()
        store(*piece).start()
    w_load.wait()
    w = wbuf[...] / jnp.sqrt(F32(16384.0))
    squares = w * w + MOMENT_EPS
    row_mean = jnp.broadcast_to(jnp.mean(squares, axis=1, keepdims=True), (256, 128))
    col_mean = jnp.mean(squares, axis=0, keepdims=True)
    row_old = jnp.broadcast_to(rowst[...], (128, 256)).T
    row_new = DECAY * row_old + (1.0 - DECAY) * row_mean
    col_new = DECAY * colst[...] + (1.0 - DECAY) * col_mean
    rown[...] = row_new.T[0:1]
    coln[...] = col_new
    row_one = row_new[:, 0:1]
    average = jnp.mean(row_one, axis=0, keepdims=True)
    upd[...] = w * lax.rsqrt(row_one * col_new / average)
    for piece in pieces:
        store(*piece).wait()


def shards(queries, keys, values, out_grad, inputs, row_state, col_state):
    hbm = pl.BlockSpec(memory_space=pl.ANY)
    vmem = pl.BlockSpec(memory_space=pltpu.VMEM)
    dma = pltpu.SemaphoreType.DMA
    scratch = [
        pltpu.VMEM((4, HEADS, TOK, 128), F32),
        pltpu.VMEM((HEADS, TOK, 128), F32),
        pltpu.VMEM((HEADS, TOK, 128), F32),
        pltpu.VMEM((2 * HEADS, 128, TOK), F32),
        pltpu.VMEM((2 * HEADS, 128, 3 * TOK), BF16),
        pltpu.VMEM((4, TOK, 512), F32),
        pltpu.VMEM((3 * TOK, 2 * PART), BF16),
        pltpu.VMEM((HEADS, NCH, 128, 128), F32),
        pltpu.VMEM((HEADS, NCH, 128, 128), F32),
        pltpu.VMEM((2, HEADS, 128, 128), F32),
        pltpu.VMEM((2, 3, 128, 128), F32),
        pltpu.VMEM((2, 4, 128, 128), F32),
        pltpu.VMEM((2, 128, 128), F32),
        pltpu.VMEM((2, 3, 128, 128), F32),
        pltpu.VMEM((2, HEADS, 128, 128), F32),
        pltpu.VMEM((JOBS, 4, 4, 64, PART), F32),
        pltpu.VMEM((JOBS, 2, 2, 64, PART), F32),
        pltpu.VMEM((JOBS, 2, 4, 64, PART), F32),
        pltpu.VMEM((JOBS, 3, 64, PART), F32),
        pltpu.VMEM((JOBS, 2, 64, PART), F32),
        pltpu.VMEM((4, 64, 512), F32),
        dma((4, HEADS)),
        dma,
        dma((2, 2, 2)),
        dma((2, 2, 2)),
        dma((2, 4)),
        dma((2, 4)),
        dma((2, 3, 3)),
        dma((2, 3, 3)),
        dma((HEADS,)),
        dma((HEADS,)),
        dma((JOBS, 8)),
        dma((JOBS, 8)),
        dma((JOBS,)),
        dma((4, 2, 2)),
        dma((2, HEADS)),
    ]
    tokens = jax.ShapeDtypeStruct((TOK, 512), F32)
    block = jax.ShapeDtypeStruct((256, 512), F32)
    query_grad, key_grad, weight_grad = pl.pallas_call(
        kernel,
        out_shape=(tokens, tokens, block),
        in_specs=[hbm] * 5,
        out_specs=(hbm, hbm, vmem),
        scratch_shapes=scratch,
        compiler_params=pltpu.CompilerParams(
            collective_id=0, has_side_effects=True, vmem_limit_bytes=60 * 1024 * 1024
        ),
        cost_estimate=pl.CostEstimate(flops=20_000_000_000, bytes_accessed=16_000_000, transcendentals=0),
    )(queries, keys, values, out_grad, inputs)
    return pl.pallas_call(
        last_kernel,
        out_shape=(
            tokens,
            tokens,
            block,
            jax.ShapeDtypeStruct((1, 256), F32),
            jax.ShapeDtypeStruct((1, 512), F32),
        ),
        in_specs=[hbm] * 3 + [vmem] * 2,
        out_specs=(hbm, hbm, vmem, vmem, vmem),
        scratch_shapes=[pltpu.VMEM((2, 4, 256, 512), F32), pltpu.VMEM((256, 512), F32), dma((2, 2, 4)), dma],
        compiler_params=pltpu.CompilerParams(vmem_limit_bytes=60 * 1024 * 1024),
        cost_estimate=pl.CostEstimate(flops=2_000_000, bytes_accessed=10_000_000, transcendentals=131072),
    )(query_grad, key_grad, weight_grad, row_state, col_state)


def solution(mesh):
    in_specs = (
        P("seq", "head"),
        P("seq", "head"),
        P("seq", "head"),
        P("seq", "head"),
        P("seq", "head"),
        P("head", "seq"),
        P("seq", "head"),
    )
    out_specs = (
        P("seq", "head"),
        P("seq", "head"),
        P("seq", "head"),
        P("head", "seq"),
        P("seq", "head"),
    )
    return jax.shard_map(shards, mesh=mesh, in_specs=in_specs, out_specs=out_specs, check_vma=False)
```
